256 devices in a mesh: pole: 4 (over y_lo, core), grid: 64 (over x, y_hi, z).
Axes of the slice: x: 4, y: 4 (y_hi: 2, y_lo: 2; y = y_hi * 2 + y_lo), z: 8, core: 2. Of those that a mesh axis runs over, the one named last changes fastest.
Arguments:
- ainv_anc: bfloat16 [4, 2, 1024, 1024], P('pole', None, 'grid'), may hold values from -6 to 6
- lower_panels: bfloat16 [4, 2, 1024, 16384], P('pole', None, None, 'grid'), may hold values from -0.125 to 0.125
- fill_pattern: int32 [64, 4], P('grid'), may hold values 0 or 1
- diag_inverse: bfloat16 [4, 2, 256, 16384], P('pole', None, None, 'grid'), may hold values from -6 to 6
- pole_weights: float32 [4, 2], P('pole'), may hold values from -4 to 4
- hamiltonian: bfloat16 [1280, 16384], P(None, 'grid'), may hold values from -0.15625 to 0.15625
- margin: bfloat16 [1280, 16384], P(None, 'grid'), may hold values from -0.15625 to 0.15625
- dft_column: int32 [16384], replicated, may hold values from 0 to 16383, as said below
Outputs:
- ainv_off: bfloat16 [4, 2, 1024, 16384], P('pole', None, None, 'grid')
- ainv_diag: bfloat16 [4, 2, 256, 16384], P('pole', None, None, 'grid')
- charges: float32 [16384], P('grid')
- band_energy: float32 [16384], P('grid')
The draws below stay inside these ranges and needn't reach their ends.
Inputs may be any that keep to these rules, and one draw needn't show every extreme that they name: dft_column is a permutation of the 16384 columns. The 256 columns that one index of grid holds, columns g * 256 to (g + 1) * 256 - 1, land on exactly 32 indices of grid in the column order, exactly 8 on each.
All inputs are finite; a program needn't handle non-finite values. No bound on the sum of `fill_pattern` on one device may be relied on, other than what follows from the above.
Results may differ from the reference program's by a relative error of at most 0.0054.
Values may be sent and summed in bfloat16 or wider, within the bound.
No kernel may reach another device: no remote copies, remote signals or barrier semaphores. Data moves between devices by JAX's collectives and lax.ppermute only.
A program may use at most 64 MiB of HBM per device.

```python
import jax
import jax.numpy as jnp

BLOCK = 256
SEPARATOR = 4
ANC = 1024
ROWS = 1280
COL_DEV = 256
NCOL = 16384
LEVEL = 64
CAP = 8
POLES = 4


def shuffle_cols(sub_key):
    return jax.random.permutation(sub_key, COL_DEV)


def draw_dft_column(key, part):
    key = jax.random.fold_in(key, 7)
    key_offset, key_source, key_target = jax.random.split(key, 3)
    groups = NCOL // COL_DEV
    senders = COL_DEV // CAP
    offsets = jax.random.permutation(key_offset, groups)[:senders].astype(jnp.int32)
    source_perm = jax.vmap(shuffle_cols)(jax.random.split(key_source, groups)).astype(jnp.int32)
    target_perm = jax.vmap(shuffle_cols)(jax.random.split(key_target, groups)).astype(jnp.int32)
    column = jnp.arange(NCOL, dtype=jnp.int32)
    source = column // COL_DEV
    within = column % COL_DEV
    ranked = source_perm[source, within]
    sender_index = ranked // CAP
    pair_slot = ranked % CAP
    target = (source + offsets[sender_index]) % groups
    landing = target_perm[target, sender_index * CAP + pair_slot]
    return (target * COL_DEV + landing).astype(jnp.int32)


def plant(entries, key, least, top_value):
    place = [jax.random.randint(jax.random.fold_in(key, axis), (), 0, length) for axis, length in enumerate(entries.shape)]
    widest = entries.shape.index(max(entries.shape))
    next_to = place[:widest] + [(place[widest] + 1) % entries.shape[widest]] + place[widest + 1:]
    return entries.at[tuple(place)].set(least).at[tuple(next_to)].set(top_value)


def steps_of(stream_key, extent, pieces, least, high):
    def one(dim, parts):
        draws = jax.random.uniform(jax.random.fold_in(jax.random.fold_in(stream_key, 6), dim), (parts,), jnp.float32, least / len(pieces), high / len(pieces))
        return jnp.repeat(jnp.exp(draws), extent[dim] // parts).reshape((-1,) + (1,) * (len(extent) - dim - 1))

    gain = one(*pieces[0])
    for cut in pieces[1:]:
        gain = gain * one(*cut)
    return gain


def centred(rng, shape, deviation, reach, cuts=(), held_as=jnp.bfloat16):
    entries = jax.random.normal(rng, shape, jnp.float32) * deviation
    if len(cuts) > 0:
        entries = steps_of(rng, shape, cuts, -0.22, 0.18) * entries
    return jnp.clip(entries, min=-reach, max=reach).astype(held_as)


def setup_inputs(seed: int = 0) -> dict:
    keys = jax.random.split(jax.random.key(seed), 9)
    return {
        "ainv_anc": centred(keys[0], (POLES, 2, ANC, ANC), 1.0, 6.0, ((0, 4), (2, 64))),
        "lower_panels": centred(keys[1], (POLES, 2, ANC, NCOL), (2 * ANC) ** -0.5, 0.125, ((0, 4), (3, 64))),
        "fill_pattern": plant((jax.random.randint(keys[2], (LEVEL, SEPARATOR), 0, 3) < 2).astype(jnp.int32), jax.random.fold_in(keys[2], 1), 0, 1),
        "diag_inverse": centred(keys[3], (POLES, 2, BLOCK, NCOL), 1.0, 6.0, ((0, 4), (3, 64))),
        "pole_weights": centred(keys[4], (POLES, 2), 1.0, 4.0, ((0, 4),), jnp.float32),
        "hamiltonian": centred(keys[5], (ROWS, NCOL), ROWS ** -0.5, 0.15625, ((1, 64),)),
        "margin": centred(keys[6], (ROWS, NCOL), ROWS ** -0.5, 0.15625, ((1, 64),)),
        "dft_column": draw_dft_column(jax.random.fold_in(keys[8], 71), 0),
    }


def complex_rows(ainv_real, ainv_imag, stacked, local_cols):
    first_product = jnp.dot(ainv_real, stacked, preferred_element_type=jnp.float32)
    second_product = jnp.dot(ainv_imag, stacked, preferred_element_type=jnp.float32)
    real_part = first_product[:, :local_cols] - second_product[:, local_cols:]
    imag_part = first_product[:, local_cols:] + second_product[:, :local_cols]
    return real_part, imag_part


def contract(left_side, right_side):
    return jnp.einsum("mkb,mkc->kbc", left_side, right_side)


def flatten_blocks(values):
    supernodes, block_size, block_cols = values.shape
    return values.transpose(1, 0, 2).reshape(block_size, supernodes * block_cols)


def reference(ainv_anc, lower_panels, fill_pattern, diag_inverse, pole_weights, hamiltonian, margin, dft_column):
    mask_low = jnp.repeat(jnp.repeat(fill_pattern.T, BLOCK, axis=0), BLOCK, axis=1).astype(jnp.bfloat16)
    mask_float = mask_low.astype(jnp.float32)
    density = jnp.zeros((ROWS, NCOL), jnp.float32)
    upper_list = []
    diag_list = []
    for pole in range(POLES):
        lower = lower_panels[pole] * mask_low[None]
        stacked = jnp.concatenate([lower[0], lower[1]], axis=1)
        real_part, imag_part = complex_rows(ainv_anc[pole, 0], ainv_anc[pole, 1], stacked, NCOL)
        upper = (-jnp.stack([real_part, imag_part]) * mask_float[None]).astype(jnp.bfloat16)
        lower_split = lower.astype(jnp.float32).reshape(2, ANC, LEVEL, BLOCK)
        upper_float = upper.astype(jnp.float32)
        upper_split = upper_float.reshape(2, ANC, LEVEL, BLOCK)
        real_diag = contract(lower_split[0], upper_split[0]) - contract(lower_split[1], upper_split[1])
        imag_diag = contract(lower_split[0], upper_split[1]) + contract(lower_split[1], upper_split[0])
        diag = diag_inverse[pole].astype(jnp.float32) - jnp.stack([flatten_blocks(real_diag), flatten_blocks(imag_diag)])
        weight_real = pole_weights[pole, 0]
        weight_imag = pole_weights[pole, 1]
        own_rows = weight_real * diag[1] + weight_imag * diag[0]
        far_rows = weight_real * upper_float[1] + weight_imag * upper_float[0]
        density = density + jnp.concatenate([own_rows, far_rows], axis=0)
        upper_list.append(upper)
        diag_list.append(diag.astype(jnp.bfloat16))
    placed = jnp.zeros((ROWS, NCOL), jnp.float32).at[:, dft_column].set(density)
    charges = jnp.sum(placed * margin.astype(jnp.float32), axis=0)
    band_energy = jnp.sum(placed * hamiltonian.astype(jnp.float32), axis=0)
    return jnp.stack(upper_list), jnp.stack(diag_list), charges, band_energy
```

```python
import functools

import jax
import jax.numpy as jnp
from jax import lax
from jax.experimental import pallas as pl
from jax.experimental.pallas import tpu as pltpu
from jax.sharding import PartitionSpec as P

F32 = jnp.float32
BF16 = jnp.bfloat16
I32 = jnp.int32
NX, NY, NZ = 4, 2, 8
GROUPS = NX * NY * NZ
POLES = 4
CAP = 8
SLOTS = GROUPS * CAP
COLS = 256
ANC = 1024
ROWS = 1280
QUARTER = ROWS // POLES
SHARD = ANC // GROUPS
VMEM_LIMIT = 50 * 1024 * 1024
SMEM_SPEC = pl.BlockSpec(memory_space=pltpu.SMEM)
VMEM_SPEC = pl.BlockSpec(memory_space=pltpu.VMEM)


def params():
    return pltpu.CompilerParams(vmem_limit_bytes=VMEM_LIMIT)


def mm(a, b, contract=((1,), (0,))):
    return lax.dot_general(a, b, (contract, ((), ())), preferred_element_type=F32)


def iota(shape, dim):
    return lax.broadcasted_iota(I32, shape, dim)


def flag(condition):
    return jnp.where(condition, 1.0, 0.0).astype(BF16)


def split_matmul(values, onehot, contract):
    high = values.astype(BF16)
    rest = values - high.astype(F32)
    middle = rest.astype(BF16)
    low = (rest - middle.astype(F32)).astype(BF16)
    return mm(high, onehot, contract) + mm(middle, onehot, contract) + mm(low, onehot, contract)


def pack_kernel(index, dft, margin, hamiltonian, out, slot_onehot):
    entries = dft[...]
    side = entries.shape[0]
    hit = (entries >> 8) == index[1]
    row, col = iota((side, side), 0), iota((side, side), 1)
    hit_flag = flag(hit)
    rank = mm(hit_flag, flag(row < col))
    previous = mm(flag(((row & 1) == 1) & (col == row - 1)), hit_flag).astype(BF16)
    rank = rank + mm(previous, jnp.ones((side, side), BF16))
    place = ((entries & 255) + 1).astype(F32)
    pair = flag((iota((GROUPS, side), 1) >> 1) == iota((GROUPS, side), 0))
    target = (iota((GROUPS, COLS), 1) + 1).astype(F32)
    pieces = []
    for r in range(CAP):
        picked = jnp.where(hit & (rank == float(r)), place, 0.0).astype(BF16)
        local = jnp.sum(mm(pair, picked), axis=1, keepdims=True)
        pieces.append(flag(local == target))
    by_rank = jnp.concatenate(pieces, axis=0)
    s, t = iota((SLOTS, SLOTS), 0), iota((SLOTS, SLOTS), 1)
    order = flag((s & (CAP - 1)) * GROUPS + (s >> 3) == t)
    onehot = mm(order, by_rank).astype(BF16)
    slot_onehot[...] = onehot
    both = jnp.concatenate([margin[...], hamiltonian[...]], axis=0)
    out[...] = mm(onehot, both, ((1,), (1,))).astype(BF16)


def pack(index, dft, margin, hamiltonian):
    quarter = pl.BlockSpec((QUARTER, COLS), lambda i, index: (index[0], 0))
    whole = lambda *shape: pl.BlockSpec(shape, lambda i, index: (0,) * len(shape))
    return pl.pallas_call(
        pack_kernel,
        grid_spec=pltpu.PrefetchScalarGridSpec(
            num_scalar_prefetch=1,
            grid=(1,),
            in_specs=[whole(*dft.shape), quarter, quarter],
            out_specs=[whole(SLOTS, 2 * QUARTER), whole(SLOTS, COLS)],
        ),
        out_shape=[
            jax.ShapeDtypeStruct((SLOTS, 2 * QUARTER), BF16),
            jax.ShapeDtypeStruct((SLOTS, COLS), BF16),
        ],
        compiler_params=params(),
        name="pack",
    )(index, dft, margin, hamiltonian)


def unpack_kernel(own_col, own_row, arrived, out, column_onehot):
    group_col, group_row = own_col[...] >> 8, own_row[...] >> 8
    before = iota((COLS, COLS), 0) < iota((COLS, COLS), 1)
    rank = jnp.sum(jnp.where((group_col == group_row) & before, 1, 0), axis=0, keepdims=True)
    slot = group_row * CAP + rank
    onehot = flag(iota((SLOTS, COLS), 0) == slot)
    column_onehot[...] = onehot
    out[...] = mm(arrived[...], onehot, ((0,), (0,))).astype(BF16)


def unpack(own_col, own_row, arrived):
    return pl.pallas_call(
        unpack_kernel,
        in_specs=[VMEM_SPEC] * 3,
        out_specs=[VMEM_SPEC] * 2,
        out_shape=[
            jax.ShapeDtypeStruct((2 * QUARTER, COLS), BF16),
            jax.ShapeDtypeStruct((SLOTS, COLS), BF16),
        ],
        compiler_params=params(),
        name="unpack",
    )(own_col, own_row, arrived)


def factor_kernel(index, weights, fill, lower, diag_inverse, own, mate, others, out, base, rows, masked):
    pole = index[0]
    for part in range(2):
        for block in range(ANC // COLS):
            keep = fill[0, block].astype(F32).astype(BF16)
            span = slice(block * COLS, (block + 1) * COLS)
            masked[part, span, :] = lower[part, span, :] * keep
    pieces = [own[...], mate[...], others[0], others[1]]
    for shift, piece in enumerate(pieces):
        start = pl.multiple_of((pole ^ shift) * QUARTER, QUARTER)
        for which in range(2):
            rows[which, pl.ds(start, QUARTER), :] = piece[which * QUARTER : (which + 1) * QUARTER, :]
    real, imag = weights[0, 0], weights[0, 1]
    for which in range(2):
        near = rows[which, 0:COLS, :]
        near_float = near.astype(F32)
        sums = real * diag_inverse[1].astype(F32) + imag * diag_inverse[0].astype(F32)
        base[which : which + 1, :] = jnp.sum(sums * near_float, axis=0, keepdims=True)
        for block in range(ANC // COLS):
            span = slice(block * COLS, (block + 1) * COLS)
            far = rows[which, (block + 1) * COLS : (block + 2) * COLS, :].astype(F32)
            direct = far - mm(masked[0, span, :], near)
            cross = mm(masked[1, span, :], near)
            out[2 * which, span, :] = imag * direct - real * cross
            out[2 * which + 1, span, :] = real * direct + imag * cross
    base[2:8, :] = jnp.zeros((6, COLS), F32)


def factors(index, weights, fill, lower, diag_inverse, own, mate, others):
    return pl.pallas_call(
        factor_kernel,
        in_specs=[SMEM_SPEC] * 3 + [VMEM_SPEC] * 5,
        out_specs=[VMEM_SPEC] * 2,
        out_shape=[
            jax.ShapeDtypeStruct((4, ANC, COLS), F32),
            jax.ShapeDtypeStruct((8, COLS), F32),
        ],
        scratch_shapes=[pltpu.VMEM((2, ROWS, COLS), BF16), pltpu.VMEM((2, ANC, COLS), BF16)],
        compiler_params=params(),
        name="factors",
    )(index, weights, fill, lower, diag_inverse, own, mate, others)


def upper_kernel(index, fill, lower, first, first_y, second, s1, s2, s3, factor, base, onehot, out, slots, both):
    grid = index[1]
    x, y, z = grid >> 4, (grid >> 3) & 1, grid & 7
    for block in range(ANC // COLS):
        keep = fill[0, block].astype(F32).astype(BF16)
        span = slice(block * COLS, (block + 1) * COLS)
        for part in range(2):
            both[span, part * COLS : (part + 1) * COLS] = lower[part, span, :] * keep
    rhs = both[...]

    def store(pair, places):
        left = mm(pair[0], rhs)
        right = mm(pair[1], rhs)
        real = right[:, COLS:] - left[:, :COLS]
        imag = -left[:, COLS:] - right[:, :COLS]
        for n, (px, py, pz) in enumerate(places):
            keep = fill[0, px].astype(F32)
            start = pl.multiple_of(px * (NY * NZ * SHARD) + py * (NZ * SHARD) + pz * SHARD, SHARD)
            span = slice(n * SHARD, (n + 1) * SHARD)
            out[0, pl.ds(start, SHARD), :] = (real[span] * keep).astype(BF16)
            out[1, pl.ds(start, SHARD), :] = (imag[span] * keep).astype(BF16)

    half = NZ // 2
    for dy, ref in ((0, first), (1, first_y)):
        pair = [ref[:, part].reshape(NX * half * SHARD, ANC) for part in range(2)]
        store(pair, [((x - dx) & 3, (y - dy) & 1, (z - k) & 7) for dx in range(NX) for k in range(half)])
    for dx, ref in enumerate((second, s1, s2, s3)):
        pair = [ref[:, part].reshape(NY * half * SHARD, ANC) for part in range(2)]
        store(pair, [((x - dx) & 3, (y - dy) & 1, (z - k) & 7) for dy in range(NY) for k in range(half, NZ)])
    rows = [base[which : which + 1, :] for which in range(2)]
    for block in range(ANC // COLS):
        span = slice(block * COLS, (block + 1) * COLS)
        real, imag = out[0, span, :].astype(F32), out[1, span, :].astype(F32)
        for which in range(2):
            term = real * factor[2 * which, span, :] + imag * factor[2 * which + 1, span, :]
            rows[which] = rows[which] + jnp.sum(term, axis=0, keepdims=True)
    values = jnp.concatenate(rows + [jnp.zeros((6, COLS), F32)], axis=0)
    slots[...] = split_matmul(values, onehot[...], ((1,), (1,)))


def upper_rows(index, fill, lower, pieces, factor, base, onehot):
    return pl.pallas_call(
        upper_kernel,
        in_specs=[SMEM_SPEC] * 2 + [VMEM_SPEC] * (4 + len(pieces)),
        out_specs=[VMEM_SPEC] * 2,
        out_shape=[
            jax.ShapeDtypeStruct((2, ANC, COLS), BF16),
            jax.ShapeDtypeStruct((8, SLOTS), F32),
        ],
        scratch_shapes=[pltpu.VMEM((ANC, 2 * COLS), BF16)],
        compiler_params=params(),
        name="upper",
    )(index, fill, lower, *pieces, factor, base, onehot)


def diag_kernel(fill, lower, upper, diag_inverse, out):
    real = diag_inverse[0].astype(F32)
    imag = diag_inverse[1].astype(F32)
    turn = ((0,), (0,))
    for block in range(ANC // COLS):
        keep = fill[0, block].astype(F32).astype(BF16)
        span = slice(block * COLS, (block + 1) * COLS)
        low_real, low_imag = lower[0, span, :] * keep, lower[1, span, :] * keep
        up_real, up_imag = upper[0, span, :], upper[1, span, :]
        real = real - mm(low_real, up_real, turn) + mm(low_imag, up_imag, turn)
        imag = imag - mm(low_real, up_imag, turn) - mm(low_imag, up_real, turn)
    out[0] = real.astype(BF16)
    out[1] = imag.astype(BF16)


def diag_block(fill, lower, upper, diag_inverse):
    return pl.pallas_call(
        diag_kernel,
        in_specs=[SMEM_SPEC] + [VMEM_SPEC] * 3,
        out_specs=VMEM_SPEC,
        out_shape=jax.ShapeDtypeStruct((2, COLS, COLS), BF16),
        compiler_params=params(),
        name="diag",
    )(fill, lower, upper, diag_inverse)


def place_kernel(slots, onehot, out):
    out[...] = split_matmul(slots[...], onehot[...], ((1,), (0,)))


def place(slots, onehot):
    return pl.pallas_call(
        place_kernel,
        in_specs=[VMEM_SPEC] * 2,
        out_specs=VMEM_SPEC,
        out_shape=jax.ShapeDtypeStruct((2, COLS), F32),
        compiler_params=params(),
        name="place",
    )(slots, onehot)


def position(x, y, z):
    return ((x % NX) * NY + y % NY) * NZ + z % NZ


def shift(value, dx=0, dy=0, dz=0):
    pairs = [
        (position(x, y, z), position(x + dx, y + dy, z + dz))
        for x in range(NX)
        for y in range(NY)
        for z in range(NZ)
    ]
    return lax.ppermute(value, "grid", pairs)


def swap_pole(value, bit):
    return lax.ppermute(value, "pole", [(p, p ^ bit) for p in range(POLES)])


def body(ainv_anc, lower_panels, fill_pattern, diag_inverse, pole_weights, hamiltonian, margin, dft_column):
    index = jnp.stack([lax.axis_index("pole"), lax.axis_index("grid")]).astype(I32)
    lower, inverse = lower_panels[0], diag_inverse[0]
    shard = ainv_anc[0]

    along = [shard] + [shift(shard, dz=k) for k in range(1, NZ)]
    first = jnp.concatenate(along[: NZ // 2], axis=1)
    second = jnp.concatenate(along[NZ // 2 :], axis=1)
    first = jnp.stack([first] + [shift(first, dx=d) for d in range(1, NX)])
    second = jnp.stack([second, shift(second, dy=1)])
    first_y = shift(first, dy=1)
    others = [shift(second, dx=d) for d in range(1, NX)]

    table = dft_column.reshape(128, 128)
    packed, slot_onehot = pack(index, table, margin, hamiltonian)
    arrived = lax.all_to_all(packed, "grid", split_axis=0, concat_axis=0, tiled=True)
    own = lax.dynamic_slice_in_dim(table, 2 * index[1], 2, 0)
    mine, column_onehot = unpack(own.reshape(COLS, 1), own.reshape(1, COLS), arrived)
    mate = swap_pole(mine, 1)
    far = swap_pole(jnp.stack([mine, mate]), 2)
    factor, base = factors(index, pole_weights, fill_pattern, lower, inverse, mine, mate, far)

    upper, slots = upper_rows(
        index, fill_pattern, lower, [first, first_y, second] + others, factor, base, column_onehot
    )
    diag = diag_block(fill_pattern, lower, upper, inverse)
    total = lax.psum(slots[:2], "pole")
    outgoing = total.reshape(2, GROUPS, CAP).transpose(1, 0, 2).reshape(GROUPS, 2 * CAP)
    incoming = lax.all_to_all(outgoing, "grid", split_axis=0, concat_axis=0, tiled=True)
    incoming = incoming.reshape(GROUPS, 2, CAP).transpose(1, 0, 2).reshape(2, SLOTS)
    placed = place(incoming, slot_onehot)
    return (upper[None], diag[None], placed[0], placed[1])


def solution(mesh):
    return jax.shard_map(
        body,
        mesh=mesh,
        in_specs=(
            P("pole", None, "grid", None),
            P("pole", None, None, "grid"),
            P("grid", None),
            P("pole", None, None, "grid"),
            P("pole", None),
            P(None, "grid"),
            P(None, "grid"),
            P(),
        ),
        out_specs=(
            P("pole", None, None, "grid"),
            P("pole", None, None, "grid"),
            P("grid"),
            P("grid"),
        ),
        check_vma=False,
    )
```

```python
import jax
import jax.numpy as jnp
from jax import lax
from jax.experimental import pallas as pl
from jax.experimental.pallas import tpu as pltpu
from jax.sharding import PartitionSpec as P

F32 = jnp.float32
BF16 = jnp.bfloat16
I32 = jnp.int32
NX, NY, NZ = 4, 2, 8
GROUPS = NX * NY * NZ
POLES = 4
CAP = 8
SLOTS = GROUPS * CAP
PLANE = NY * NZ
COLS = 256
ANC = 1024
ROWS = 1280
QUARTER = ROWS // POLES
SHARD = ANC // GROUPS
LATE = 384
EARLY = ANC - LATE
VMEM_LIMIT = 50 * 1024 * 1024
SMEM_SPEC = pl.BlockSpec(memory_space=pltpu.SMEM)
VMEM_SPEC = pl.BlockSpec(memory_space=pltpu.VMEM)
ANY_SPEC = pl.BlockSpec(memory_space=pl.ANY)


def params():
    return pltpu.CompilerParams(vmem_limit_bytes=VMEM_LIMIT)


def mm(a, b, contract=((1,), (0,))):
    return lax.dot_general(a, b, (contract, ((), ())), preferred_element_type=F32)


def iota(shape, dim):
    return lax.broadcasted_iota(I32, shape, dim)


def flag(condition):
    return jnp.where(condition, 1.0, 0.0).astype(BF16)


def split_matmul(values, onehot, contract):
    high = values.astype(BF16)
    rest = values - high.astype(F32)
    middle = rest.astype(BF16)
    low = (rest - middle.astype(F32)).astype(BF16)
    return mm(high, onehot, contract) + mm(middle, onehot, contract) + mm(low, onehot, contract)


def pack_kernel(index, dft, margin, hamiltonian, out0, out1, out2, out3, slot_onehot, both, sems):
    start = pl.multiple_of(index[0] * QUARTER, QUARTER)
    copies = [
        pltpu.make_async_copy(ref.at[pl.ds(start, QUARTER), :], both.at[pl.ds(n * QUARTER, QUARTER), :], sems.at[n])
        for n, ref in enumerate((margin, hamiltonian))
    ]
    for copy in copies:
        copy.start()
    entries = dft[...]
    side = entries.shape[0]
    hit = (entries >> 8) == index[1]
    row, col = iota((side, side), 0), iota((side, side), 1)
    hit_flag = flag(hit)
    rank = mm(hit_flag, flag(row < col))
    previous = mm(flag(((row & 1) == 1) & (col == row - 1)), hit_flag).astype(BF16)
    rank = rank + mm(previous, jnp.ones((side, side), BF16))
    place = ((entries & 255) + 1).astype(F32)
    pair = flag((iota((GROUPS, side), 1) >> 1) == iota((GROUPS, side), 0))
    target = (iota((GROUPS, COLS), 1) + 1).astype(F32)
    pieces = []
    for r in range(CAP):
        picked = jnp.where(hit & (rank == float(r)), place, 0.0).astype(BF16)
        local = jnp.sum(mm(pair, picked), axis=1, keepdims=True)
        pieces.append(flag(local == target))
    by_rank = jnp.concatenate(pieces, axis=0)
    s, t = iota((SLOTS, SLOTS), 0), iota((SLOTS, SLOTS), 1)
    order = flag((s & (CAP - 1)) * GROUPS + (s >> 3) == t)
    slot_onehot[...] = mm(order, by_rank).astype(BF16)
    for copy in copies:
        copy.wait()
    rows = both[...]
    x = index[1] >> 4
    for turn, out in enumerate((out0, out1, out2, out3)):
        first = pl.multiple_of(((x + turn) & (NX - 1)) * (PLANE * CAP), PLANE * CAP)
        out[...] = mm(slot_onehot[pl.ds(first, PLANE * CAP), :], rows, ((1,), (1,))).astype(BF16)


def pack(index, dft, margin, hamiltonian):
    return pl.pallas_call(
        pack_kernel,
        in_specs=[SMEM_SPEC, VMEM_SPEC, ANY_SPEC, ANY_SPEC],
        out_specs=[VMEM_SPEC] * (NX + 1),
        out_shape=[jax.ShapeDtypeStruct((PLANE * CAP, 2 * QUARTER), BF16)] * NX
        + [jax.ShapeDtypeStruct((SLOTS, COLS), BF16)],
        scratch_shapes=[pltpu.VMEM((2 * QUARTER, COLS), BF16), pltpu.SemaphoreType.DMA((2,))],
        compiler_params=params(),
        name="pack",
    )(index, dft, margin, hamiltonian)


def unpack_kernel(index, dft, arrived, out, column_onehot):
    grid = index[1]
    group_row = jnp.concatenate([dft[pl.ds(2 * grid, 1), :], dft[pl.ds(2 * grid + 1, 1), :]], axis=1) >> 8
    above, across = iota((COLS, COLS), 0), iota((COLS, COLS), 1)
    group_col = jnp.sum(jnp.where(above == across, group_row, 0), axis=1, keepdims=True)
    rank = jnp.sum(jnp.where((group_col == group_row) & (above < across), 1, 0), axis=0, keepdims=True)
    place = iota((SLOTS, COLS), 0)
    column_onehot[...] = flag(place == group_row * CAP + rank)
    turn = ((grid >> 4) - (group_row >> 4)) & (NX - 1)
    slot = (group_row & (PLANE - 1)) * (NX * CAP) + turn * CAP + rank
    out[...] = mm(arrived[...], flag(place == slot), ((0,), (0,))).astype(BF16)


def unpack(index, dft, arrived):
    return pl.pallas_call(
        unpack_kernel,
        in_specs=[SMEM_SPEC] + [VMEM_SPEC] * 2,
        out_specs=[VMEM_SPEC] * 2,
        out_shape=[
            jax.ShapeDtypeStruct((2 * QUARTER, COLS), BF16),
            jax.ShapeDtypeStruct((SLOTS, COLS), BF16),
        ],
        compiler_params=params(),
        name="unpack",
    )(index, dft, arrived)


def factor_kernel(index, weights, fill, lower, diag_inverse, own, mates, out, base, rows, masked):
    pole = index[0]
    for part in range(2):
        for block in range(ANC // COLS):
            keep = fill[0, block].astype(F32).astype(BF16)
            span = slice(block * COLS, (block + 1) * COLS)
            masked[part, span, :] = lower[part, span, :] * keep
    for bits, ref, n in ((0, own, 0), (2, own, 1), (1, mates, 0), (3, mates, 1)):
        start = pl.multiple_of((pole ^ bits) * QUARTER, QUARTER)
        for which in range(2):
            rows[which, pl.ds(start, QUARTER), :] = ref[n, which * QUARTER : (which + 1) * QUARTER, :]
    real, imag = weights[0, 0], weights[0, 1]
    for which in range(2):
        near = rows[which, 0:COLS, :]
        near_float = near.astype(F32)
        sums = real * diag_inverse[1].astype(F32) + imag * diag_inverse[0].astype(F32)
        base[which : which + 1, :] = jnp.sum(sums * near_float, axis=0, keepdims=True)
        for block in range(ANC // COLS):
            span = slice(block * COLS, (block + 1) * COLS)
            far = rows[which, (block + 1) * COLS : (block + 2) * COLS, :].astype(F32)
            direct = far - mm(masked[0, span, :], near)
            cross = mm(masked[1, span, :], near)
            out[2 * which, span, :] = imag * direct - real * cross
            out[2 * which + 1, span, :] = real * direct + imag * cross
    base[2:8, :] = jnp.zeros((6, COLS), F32)


def factors(index, weights, fill, lower, diag_inverse, own, mates):
    return pl.pallas_call(
        factor_kernel,
        in_specs=[SMEM_SPEC] * 3 + [VMEM_SPEC] * 4,
        out_specs=[VMEM_SPEC] * 2,
        out_shape=[
            jax.ShapeDtypeStruct((4, ANC, COLS), F32),
            jax.ShapeDtypeStruct((8, COLS), F32),
        ],
        scratch_shapes=[pltpu.VMEM((2, ROWS, COLS), BF16), pltpu.VMEM((2, ANC, COLS), BF16)],
        compiler_params=params(),
        name="factors",
    )(index, weights, fill, lower, diag_inverse, own, mates)


def upper_kernel(index, fill, lower, *refs):
    early, late, (factor, base, onehot, out, slots, both, real_sum, imag_sum) = refs[:6], refs[6:10], refs[10:]
    first, first_y, second, second_x1, second_x2, second_x3 = early
    grid = index[1]
    x, y, z = grid >> 4, (grid >> 3) & 1, grid & 7
    for block in range(ANC // COLS):
        keep = fill[0, block].astype(F32).astype(BF16)
        span = slice(block * COLS, (block + 1) * COLS)
        for part in range(2):
            both[span, part * COLS : (part + 1) * COLS] = lower[part, span, :] * keep

    def product(ref, rhs):
        left, right = [mm(ref[:, part].reshape(-1, ref.shape[-1]), rhs) for part in range(2)]
        return right[:, COLS:] - left[:, :COLS], -left[:, COLS:] - right[:, :COLS]

    def start_of(dx, dy, dz):
        px, py, pz = (x - dx) & (NX - 1), (y - dy) & (NY - 1), (z - dz) & (NZ - 1)
        return pl.multiple_of(((px * NY + py) * NZ + pz) * SHARD, SHARD)

    def scatter(ref, places):
        real, imag = product(ref, both[0:EARLY, :])
        for n, place in enumerate(places):
            span = slice(n * SHARD, (n + 1) * SHARD)
            start = start_of(*place)
            real_sum[pl.ds(start, SHARD), :] = real[span]
            imag_sum[pl.ds(start, SHARD), :] = imag[span]

    for dy, ref in ((0, first), (1, first_y)):
        scatter(ref, [(dx, dy, dz) for dx in range(NX) for dz in (0, 4, 1, 5)])
    for dx, ref in enumerate((second, second_x1, second_x2, second_x3)):
        scatter(ref, [(dx, dy, dz) for dy in range(NY) for dz in (7, 3, 2, 6)])
    rows = [base[which : which + 1, :] for which in range(2)]
    tail = both[EARLY:ANC, :]
    for n, dzs in enumerate(((0, 4), (1, 5), (7, 3), (2, 6))):
        real, imag = product(late[n], tail)
        places = [(dx, dy, dz) for dz in dzs for dy in range(NY) for dx in range(NX)]
        for m, place in enumerate(places):
            span = slice(m * SHARD, (m + 1) * SHARD)
            start = start_of(*place)
            keep = fill[0, (x - place[0]) & (NX - 1)].astype(F32)
            here = pl.ds(start, SHARD)
            out[0, here, :] = ((real[span] + real_sum[here, :]) * keep).astype(BF16)
            out[1, here, :] = ((imag[span] + imag_sum[here, :]) * keep).astype(BF16)
    for block in range(ANC // COLS):
        span = slice(block * COLS, (block + 1) * COLS)
        real, imag = out[0, span, :].astype(F32), out[1, span, :].astype(F32)
        for which in range(2):
            term = real * factor[2 * which, span, :] + imag * factor[2 * which + 1, span, :]
            rows[which] = rows[which] + jnp.sum(term, axis=0, keepdims=True)
    line = iota((8, COLS), 0)
    values = jnp.where(line == 2 * x, rows[0], jnp.where(line == 2 * x + 1, rows[1], 0.0))
    sums = split_matmul(values, onehot[...], ((1,), (1,)))
    width = PLANE * CAP
    for px in range(NX):
        for pole in range(POLES):
            slots[pole * NX + px] = sums[:, px * width : (px + 1) * width]


def upper_rows(index, fill, lower, early, late, factor, base, onehot):
    return pl.pallas_call(
        upper_kernel,
        in_specs=[SMEM_SPEC] * 2 + [VMEM_SPEC] * (4 + len(early) + len(late)),
        out_specs=[VMEM_SPEC] * 2,
        out_shape=[
            jax.ShapeDtypeStruct((2, ANC, COLS), BF16),
            jax.ShapeDtypeStruct((POLES * NX, 8, PLANE * CAP), F32),
        ],
        scratch_shapes=[
            pltpu.VMEM((ANC, 2 * COLS), BF16),
            pltpu.VMEM((ANC, COLS), F32),
            pltpu.VMEM((ANC, COLS), F32),
        ],
        compiler_params=params(),
        name="upper",
    )(index, fill, lower, *early, *late, factor, base, onehot)


def diag_kernel(fill, lower, upper, diag_inverse, out):
    real = diag_inverse[0].astype(F32)
    imag = diag_inverse[1].astype(F32)
    turn = ((0,), (0,))
    for block in range(ANC // COLS):
        keep = fill[0, block].astype(F32).astype(BF16)
        span = slice(block * COLS, (block + 1) * COLS)
        low_real, low_imag = lower[0, span, :] * keep, lower[1, span, :] * keep
        up_real, up_imag = upper[0, span, :], upper[1, span, :]
        real = real - mm(low_real, up_real, turn) + mm(low_imag, up_imag, turn)
        imag = imag - mm(low_real, up_imag, turn) - mm(low_imag, up_real, turn)
    out[0] = real.astype(BF16)
    out[1] = imag.astype(BF16)


def diag_block(fill, lower, upper, diag_inverse):
    return pl.pallas_call(
        diag_kernel,
        in_specs=[SMEM_SPEC] + [VMEM_SPEC] * 3,
        out_specs=VMEM_SPEC,
        out_shape=jax.ShapeDtypeStruct((2, COLS, COLS), BF16),
        compiler_params=params(),
        name="diag",
    )(fill, lower, upper, diag_inverse)


def turn_kernel(arrived, out):
    total = jnp.sum(arrived[...], axis=0)
    width = PLANE * CAP
    for n in range(PLANE):
        out[n] = total if n == 0 else pltpu.roll(total, width - n * CAP, 1)


def turn(arrived):
    return pl.pallas_call(
        turn_kernel,
        in_specs=[VMEM_SPEC],
        out_specs=VMEM_SPEC,
        out_shape=jax.ShapeDtypeStruct((PLANE, 8, PLANE * CAP), F32),
        compiler_params=params(),
        name="turn",
    )(arrived)


def place_kernel(arrived, onehot, out):
    width = PLANE * CAP
    line, lane = iota((8, width), 0), iota((8, width), 1)
    total = jnp.zeros((8, width), F32)
    for n in range(PLANE):
        piece = jnp.where(lane < CAP, arrived[n], 0.0)
        total = total + (piece if n == 0 else pltpu.roll(piece, n * CAP, 1))
    wide = jnp.concatenate([jnp.where((line >> 1) == px, total, 0.0) for px in range(NX)], axis=1)
    result = split_matmul(wide, onehot[...], ((1,), (0,)))
    for which in range(2):
        out[which : which + 1, :] = jnp.sum(
            jnp.where((iota((8, COLS), 0) & 1) == which, result, 0.0), axis=0, keepdims=True
        )


def place(arrived, onehot):
    return pl.pallas_call(
        place_kernel,
        in_specs=[VMEM_SPEC] * 2,
        out_specs=VMEM_SPEC,
        out_shape=jax.ShapeDtypeStruct((2, COLS), F32),
        compiler_params=params(),
        name="place",
    )(arrived, onehot)


SIZES = {"ylo": 2, "core": 2, "x": NX, "yhi": NY, "z": NZ}


def shift(value, axis, by):
    size = SIZES[axis]
    return lax.ppermute(value, axis, [(n, (n + by) % size) for n in range(size)])


def all_of_z(value):
    pair = jnp.stack([value, shift(value, "z", 4)])
    return [pair, shift(pair, "z", 1), shift(pair, "z", -1), shift(pair, "z", 2)]


def body(ainv_anc, lower_panels, fill_pattern, diag_inverse, pole_weights, hamiltonian, margin, dft_column):
    pole = lax.axis_index("ylo") * 2 + lax.axis_index("core")
    grid = (lax.axis_index("x") * NY + lax.axis_index("yhi")) * NZ + lax.axis_index("z")
    index = jnp.stack([pole, grid]).astype(I32)
    lower, inverse = lower_panels[0], diag_inverse[0]
    early, late = ainv_anc[0, :, :, :EARLY], ainv_anc[0, :, :, EARLY:]

    near, near_up, near_down, near_two = all_of_z(early)
    first = jnp.concatenate([near, near_up])
    second = jnp.concatenate([near_down, near_two])
    first = jnp.concatenate([first] + [shift(first, "x", d) for d in (1, 2, 3)])
    second = jnp.concatenate([second, shift(second, "yhi", 1)])
    first_y = shift(first, "yhi", 1)
    second_x = [shift(second, "x", d) for d in (1, 2, 3)]

    late = jnp.stack([late] + [shift(late, "x", d) for d in (1, 2, 3)])
    late = jnp.concatenate([late, shift(late, "yhi", 1)])
    late = [value.reshape(2 * NX * NY, 2, SHARD, LATE) for value in all_of_z(late)]

    table = dft_column.reshape(128, 128)
    packed = pack(index, table, margin, hamiltonian)
    slot_onehot = packed[NX]
    packed = [value.reshape(PLANE, CAP, 2 * QUARTER) for value in packed[:NX]]
    outgoing = jnp.stack([packed[0]] + [shift(packed[d], "x", d) for d in (1, 2, 3)], axis=1)
    arrived = lax.all_to_all(outgoing, ("yhi", "z"), split_axis=0, concat_axis=0, tiled=True)
    mine, column_onehot = unpack(index, table, arrived.reshape(SLOTS, 2 * QUARTER))
    mine = jnp.stack([mine, shift(mine, "ylo", 1)])
    mates = shift(mine, "core", 1)
    factor, base = factors(index, pole_weights, fill_pattern, lower, inverse, mine, mates)

    upper, slots = upper_rows(
        index, fill_pattern, lower, [first, first_y, second] + second_x, late, factor, base, column_onehot
    )
    diag = diag_block(fill_pattern, lower, upper, inverse)
    sums = lax.all_to_all(slots, ("ylo", "core", "x"), split_axis=0, concat_axis=0, tiled=True)
    sums = lax.all_to_all(turn(sums), ("yhi", "z"), split_axis=0, concat_axis=0, tiled=True)
    placed = place(sums, slot_onehot)
    return (upper[None], diag[None], placed[0], placed[1])


def solution(mesh):
    fine = jax.sharding.Mesh(mesh.devices.reshape(2, 2, NX, NY, NZ), ("ylo", "core", "x", "yhi", "z"))
    pole, grid = ("ylo", "core"), ("x", "yhi", "z")
    return jax.shard_map(
        body,
        mesh=fine,
        in_specs=(
            P(pole, None, grid, None),
            P(pole, None, None, grid),
            P(grid, None),
            P(pole, None, None, grid),
            P(pole, None),
            P(None, grid),
            P(None, grid),
            P(),
        ),
        out_specs=(
            P(pole, None, None, grid),
            P(pole, None, None, grid),
            P(grid),
            P(grid),
        ),
        check_vma=False,
    )
```

```python
import jax
import jax.numpy as jnp
from jax import lax
from jax.experimental import pallas as pl
from jax.experimental.pallas import tpu as pltpu
from jax.sharding import PartitionSpec as P

F32 = jnp.float32
BF16 = jnp.bfloat16
I32 = jnp.int32
NX, NY, NZ = 4, 2, 8
GROUPS = NX * NY * NZ
POLES = 4
CAP = 8
SLOTS = GROUPS * CAP
PLANE = NY * NZ
COLS = 256
ANC = 1024
ROWS = 1280
QUARTER = ROWS // POLES
SHARD = ANC // GROUPS
MIB = 1024 * 1024
SMEM_SPEC = pl.BlockSpec(memory_space=pltpu.SMEM)
VMEM_SPEC = pl.BlockSpec(memory_space=pltpu.VMEM)
HBM_SPEC = pl.BlockSpec(memory_space=pltpu.HBM)


def params(mib=16):
    return pltpu.CompilerParams(vmem_limit_bytes=mib * MIB)


def mm(a, b, contract=((1,), (0,))):
    return lax.dot_general(a, b, (contract, ((), ())), preferred_element_type=F32)


def iota(shape, dim):
    return lax.broadcasted_iota(I32, shape, dim)


def flag(condition):
    return jnp.where(condition, 1.0, 0.0).astype(BF16)


def split_matmul(values, onehot, contract):
    high = values.astype(BF16)
    rest = values - high.astype(F32)
    middle = rest.astype(BF16)
    low = (rest - middle.astype(F32)).astype(BF16)
    return mm(high, onehot, contract) + mm(middle, onehot, contract) + mm(low, onehot, contract)


def pack_kernel(index, dft, margin, hamiltonian, out0, out1, out2, out3, slot_onehot, both, sems):
    start = pl.multiple_of(index[0] * QUARTER, QUARTER)
    copies = [
        pltpu.make_async_copy(ref.at[pl.ds(start, QUARTER), :], both.at[pl.ds(n * QUARTER, QUARTER), :], sems.at[n])
        for n, ref in enumerate((margin, hamiltonian))
    ]
    for copy in copies:
        copy.start()
    entries = dft[...]
    side = entries.shape[0]
    hit = (entries >> 8) == index[1]
    row, col = iota((side, side), 0), iota((side, side), 1)
    hit_flag = flag(hit)
    rank = mm(hit_flag, flag(row < col))
    previous = mm(flag(((row & 1) == 1) & (col == row - 1)), hit_flag).astype(BF16)
    rank = rank + mm(previous, jnp.ones((side, side), BF16))
    place = ((entries & 255) + 1).astype(F32)
    pair = flag((iota((GROUPS, side), 1) >> 1) == iota((GROUPS, side), 0))
    target = (iota((GROUPS, COLS), 1) + 1).astype(F32)
    pieces = []
    for r in range(CAP):
        picked = jnp.where(hit & (rank == float(r)), place, 0.0).astype(BF16)
        local = jnp.sum(mm(pair, picked), axis=1, keepdims=True)
        pieces.append(flag(local == target))
    by_rank = jnp.concatenate(pieces, axis=0)
    s, t = iota((SLOTS, SLOTS), 0), iota((SLOTS, SLOTS), 1)
    order = flag((s & (CAP - 1)) * GROUPS + (s >> 3) == t)
    slot_onehot[...] = mm(order, by_rank).astype(BF16)
    for copy in copies:
        copy.wait()
    rows = both[...]
    x = index[1] >> 4
    for turn, out in enumerate((out0, out1, out2, out3)):
        first = pl.multiple_of(((x + turn) & (NX - 1)) * (PLANE * CAP), PLANE * CAP)
        out[...] = mm(slot_onehot[pl.ds(first, PLANE * CAP), :], rows, ((1,), (1,))).astype(BF16)


def pack(index, dft, margin, hamiltonian):
    return pl.pallas_call(
        pack_kernel,
        in_specs=[SMEM_SPEC, VMEM_SPEC, HBM_SPEC, HBM_SPEC],
        out_specs=[VMEM_SPEC] * (NX + 1),
        out_shape=[jax.ShapeDtypeStruct((PLANE * CAP, 2 * QUARTER), BF16)] * NX
        + [jax.ShapeDtypeStruct((SLOTS, COLS), BF16)],
        scratch_shapes=[pltpu.VMEM((2 * QUARTER, COLS), BF16), pltpu.SemaphoreType.DMA((2,))],
        compiler_params=params(62),
        name="pack",
    )(index, dft, margin, hamiltonian)


def unpack_kernel(index, dft, arrived, out, column_onehot):
    grid = index[1]
    group_row = jnp.concatenate([dft[pl.ds(2 * grid, 1), :], dft[pl.ds(2 * grid + 1, 1), :]], axis=1) >> 8
    above, across = iota((COLS, COLS), 0), iota((COLS, COLS), 1)
    group_col = jnp.sum(jnp.where(above == across, group_row, 0), axis=1, keepdims=True)
    rank = jnp.sum(jnp.where((group_col == group_row) & (above < across), 1, 0), axis=0, keepdims=True)
    place = iota((SLOTS, COLS), 0)
    column_onehot[...] = flag(place == group_row * CAP + rank)
    turn = ((grid >> 4) - (group_row >> 4)) & (NX - 1)
    slot = (group_row & (PLANE - 1)) * (NX * CAP) + turn * CAP + rank
    out[...] = mm(arrived[...], flag(place == slot), ((0,), (0,))).astype(BF16)


def unpack(index, dft, arrived):
    return pl.pallas_call(
        unpack_kernel,
        in_specs=[SMEM_SPEC] + [VMEM_SPEC] * 2,
        out_specs=[VMEM_SPEC] * 2,
        out_shape=[
            jax.ShapeDtypeStruct((2 * QUARTER, COLS), BF16),
            jax.ShapeDtypeStruct((SLOTS, COLS), BF16),
        ],
        compiler_params=params(),
        name="unpack",
    )(index, dft, arrived)


def factor_kernel(index, weights, fill, lower, diag_inverse, own, mates, out, base, rows, masked):
    pole = index[0]
    for part in range(2):
        for block in range(ANC // COLS):
            keep = fill[0, block].astype(F32).astype(BF16)
            span = slice(block * COLS, (block + 1) * COLS)
            masked[part, span, :] = lower[part, span, :] * keep
    for bits, ref, n in ((0, own, 0), (2, own, 1), (1, mates, 0), (3, mates, 1)):
        start = pl.multiple_of((pole ^ bits) * QUARTER, QUARTER)
        for which in range(2):
            rows[which, pl.ds(start, QUARTER), :] = ref[n, which * QUARTER : (which + 1) * QUARTER, :]
    real, imag = weights[0, 0], weights[0, 1]
    for which in range(2):
        near = rows[which, 0:COLS, :]
        near_float = near.astype(F32)
        sums = real * diag_inverse[1].astype(F32) + imag * diag_inverse[0].astype(F32)
        base[which : which + 1, :] = jnp.sum(sums * near_float, axis=0, keepdims=True)
        for block in range(ANC // COLS):
            span = slice(block * COLS, (block + 1) * COLS)
            far = rows[which, (block + 1) * COLS : (block + 2) * COLS, :].astype(F32)
            direct = far - mm(masked[0, span, :], near)
            cross = mm(masked[1, span, :], near)
            out[2 * which, span, :] = imag * direct - real * cross
            out[2 * which + 1, span, :] = real * direct + imag * cross
    base[2:8, :] = jnp.zeros((6, COLS), F32)


def factors(index, weights, fill, lower, diag_inverse, own, mates):
    return pl.pallas_call(
        factor_kernel,
        in_specs=[SMEM_SPEC] * 3 + [VMEM_SPEC] * 4,
        out_specs=[VMEM_SPEC] * 2,
        out_shape=[
            jax.ShapeDtypeStruct((4, ANC, COLS), F32),
            jax.ShapeDtypeStruct((8, COLS), F32),
        ],
        scratch_shapes=[pltpu.VMEM((2, ROWS, COLS), BF16), pltpu.VMEM((2, ANC, COLS), BF16)],
        compiler_params=params(24),
        name="factors",
    )(index, weights, fill, lower, diag_inverse, own, mates)


def upper_kernel(index, fill, lower, first, first_y, second, second_1, second_2, second_3, factor, base, onehot, out, slots, both):
    grid = index[1]
    x, y, z = grid >> 4, (grid >> 3) & 1, grid & 7
    for block in range(ANC // COLS):
        keep = fill[0, block].astype(F32).astype(BF16)
        span = slice(block * COLS, (block + 1) * COLS)
        for part in range(2):
            both[span, part * COLS : (part + 1) * COLS] = lower[part, span, :] * keep

    def scatter(refs, places):
        rhs = both[...]
        left, right = [
            mm(jnp.concatenate([ref[:, part].reshape(-1, ANC) for ref in refs], axis=0), rhs) for part in range(2)
        ]
        for n, (dx, dy, dz) in enumerate(places):
            px, py, pz = (x - dx) & (NX - 1), (y - dy) & (NY - 1), (z - dz) & (NZ - 1)
            here = pl.ds(pl.multiple_of(((px * NY + py) * NZ + pz) * SHARD, SHARD), SHARD)
            keep = fill[0, px].astype(F32)
            span = slice(n * SHARD, (n + 1) * SHARD)
            out[0, here, :] = ((right[span, COLS:] - left[span, :COLS]) * keep).astype(BF16)
            out[1, here, :] = ((-left[span, COLS:] - right[span, :COLS]) * keep).astype(BF16)

    for dy, ref in ((0, first), (1, first_y)):
        scatter([ref], [(dx, dy, dz) for dx in range(NX) for dz in (0, 4, 1, 5)])
    for dx, refs in ((0, (second, second_1)), (2, (second_2, second_3))):
        scatter(refs, [(dx + n, dy, dz) for n in range(2) for dy in range(NY) for dz in (7, 3, 2, 6)])
    rows = [base[which : which + 1, :] for which in range(2)]
    for block in range(ANC // COLS):
        span = slice(block * COLS, (block + 1) * COLS)
        real, imag = out[0, span, :].astype(F32), out[1, span, :].astype(F32)
        for which in range(2):
            term = real * factor[2 * which, span, :] + imag * factor[2 * which + 1, span, :]
            rows[which] = rows[which] + jnp.sum(term, axis=0, keepdims=True)
    line = iota((8, COLS), 0)
    values = jnp.where(line == 2 * x, rows[0], jnp.where(line == 2 * x + 1, rows[1], 0.0))
    sums = split_matmul(values, onehot[...], ((1,), (1,)))
    width = PLANE * CAP
    for px in range(NX):
        for pole in range(POLES):
            slots[pole * NX + px] = sums[:, px * width : (px + 1) * width]


def upper_rows(index, fill, lower, pieces, factor, base, onehot):
    return pl.pallas_call(
        upper_kernel,
        in_specs=[SMEM_SPEC] * 2 + [VMEM_SPEC] * (4 + len(pieces)),
        out_specs=[VMEM_SPEC] * 2,
        out_shape=[
            jax.ShapeDtypeStruct((2, ANC, COLS), BF16),
            jax.ShapeDtypeStruct((POLES * NX, 8, PLANE * CAP), F32),
        ],
        scratch_shapes=[pltpu.VMEM((ANC, 2 * COLS), BF16)],
        compiler_params=params(28),
        name="upper",
    )(index, fill, lower, *pieces, factor, base, onehot)


def diag_kernel(fill, lower, upper, diag_inverse, out):
    real = diag_inverse[0].astype(F32)
    imag = diag_inverse[1].astype(F32)
    turn = ((0,), (0,))
    for block in range(ANC // COLS):
        keep = fill[0, block].astype(F32).astype(BF16)
        span = slice(block * COLS, (block + 1) * COLS)
        low_real, low_imag = lower[0, span, :] * keep, lower[1, span, :] * keep
        up_real, up_imag = upper[0, span, :], upper[1, span, :]
        real = real - mm(low_real, up_real, turn) + mm(low_imag, up_imag, turn)
        imag = imag - mm(low_real, up_imag, turn) - mm(low_imag, up_real, turn)
    out[0] = real.astype(BF16)
    out[1] = imag.astype(BF16)


def diag_block(fill, lower, upper, diag_inverse):
    return pl.pallas_call(
        diag_kernel,
        in_specs=[SMEM_SPEC] + [VMEM_SPEC] * 3,
        out_specs=VMEM_SPEC,
        out_shape=jax.ShapeDtypeStruct((2, COLS, COLS), BF16),
        compiler_params=params(),
        name="diag",
    )(fill, lower, upper, diag_inverse)


def turn_kernel(arrived, out):
    total = jnp.sum(arrived[...], axis=0)
    width = PLANE * CAP
    for n in range(PLANE):
        out[n] = total if n == 0 else pltpu.roll(total, width - n * CAP, 1)


def turn(arrived):
    return pl.pallas_call(
        turn_kernel,
        in_specs=[VMEM_SPEC],
        out_specs=VMEM_SPEC,
        out_shape=jax.ShapeDtypeStruct((PLANE, 8, PLANE * CAP), F32),
        compiler_params=params(),
        name="turn",
    )(arrived)


def place_kernel(arrived, onehot, out):
    width = PLANE * CAP
    line, lane = iota((8, width), 0), iota((8, width), 1)
    total = jnp.zeros((8, width), F32)
    for n in range(PLANE):
        piece = jnp.where(lane < CAP, arrived[n], 0.0)
        total = total + (piece if n == 0 else pltpu.roll(piece, n * CAP, 1))
    wide = jnp.concatenate([jnp.where((line >> 1) == px, total, 0.0) for px in range(NX)], axis=1)
    result = split_matmul(wide, onehot[...], ((1,), (0,)))
    for which in range(2):
        out[which : which + 1, :] = jnp.sum(
            jnp.where((iota((8, COLS), 0) & 1) == which, result, 0.0), axis=0, keepdims=True
        )


def place(arrived, onehot):
    return pl.pallas_call(
        place_kernel,
        in_specs=[VMEM_SPEC] * 2,
        out_specs=VMEM_SPEC,
        out_shape=jax.ShapeDtypeStruct((2, COLS), F32),
        compiler_params=params(),
        name="place",
    )(arrived, onehot)


SIZES = {"ylo": 2, "core": 2, "x": NX, "yhi": NY, "z": NZ}


def shift(value, axis, by):
    size = SIZES[axis]
    return lax.ppermute(value, axis, [(n, (n + by) % size) for n in range(size)])


def all_of_z(value):
    pair = jnp.stack([value, shift(value, "z", 4)])
    return [pair, shift(pair, "z", 1), shift(pair, "z", -1), shift(pair, "z", 2)]


def body(ainv_anc, lower_panels, fill_pattern, diag_inverse, pole_weights, hamiltonian, margin, dft_column):
    pole = lax.axis_index("ylo") * 2 + lax.axis_index("core")
    grid = (lax.axis_index("x") * NY + lax.axis_index("yhi")) * NZ + lax.axis_index("z")
    index = jnp.stack([pole, grid]).astype(I32)
    lower, inverse = lower_panels[0], diag_inverse[0]
    shard = ainv_anc[0]

    near, near_up, near_down, near_two = all_of_z(shard)
    first = jnp.concatenate([near, near_up])
    second = jnp.concatenate([near_down, near_two])
    first_1, first_2, first_3 = [shift(first, "x", d) for d in (1, 2, 3)]
    second_y = shift(second, "yhi", 1)
    first, second_y = lax.optimization_barrier((first, second_y))
    first = jnp.concatenate([first, first_1, first_2, first_3])
    second = jnp.concatenate([second, second_y])
    first_y = shift(first, "yhi", 1)
    second_x = [shift(second, "x", d) for d in (1, 2, 3)]

    table = dft_column.reshape(128, 128)
    table, near = lax.optimization_barrier((table, near))
    packed = pack(index, table, margin, hamiltonian)
    slot_onehot = packed[NX]
    packed = [value.reshape(PLANE, CAP, 2 * QUARTER) for value in packed[:NX]]
    outgoing = jnp.stack([packed[0]] + [shift(packed[d], "x", d) for d in (1, 2, 3)], axis=1)
    outgoing, near_up, near_down, near_two = lax.optimization_barrier((outgoing, near_up, near_down, near_two))
    arrived = lax.all_to_all(outgoing, ("yhi", "z"), split_axis=0, concat_axis=0, tiled=True)
    mine, column_onehot = unpack(index, table, arrived.reshape(SLOTS, 2 * QUARTER))
    mine = jnp.stack([mine, shift(mine, "ylo", 1)])
    mates = shift(mine, "core", 1)
    second_1, second_2, second_3 = second_x
    mates, second_1, second_2, second_3 = lax.optimization_barrier((mates, second_1, second_2, second_3))
    factor, base = factors(index, pole_weights, fill_pattern, lower, inverse, mine, mates)

    upper, slots = upper_rows(
        index, fill_pattern, lower, [first, first_y, second] + second_x, factor, base, column_onehot
    )
    diag = diag_block(fill_pattern, lower, upper, inverse)
    sums = lax.all_to_all(slots, ("ylo", "core", "x"), split_axis=0, concat_axis=0, tiled=True)
    sums = lax.all_to_all(turn(sums), ("yhi", "z"), split_axis=0, concat_axis=0, tiled=True)
    placed = place(sums, slot_onehot)
    return (upper[None], diag[None], placed[0], placed[1])


def solution(mesh):
    fine = jax.sharding.Mesh(mesh.devices.reshape(2, 2, NX, NY, NZ), ("ylo", "core", "x", "yhi", "z"))
    pole, grid = ("ylo", "core"), ("x", "yhi", "z")
    return jax.shard_map(
        body,
        mesh=fine,
        in_specs=(
            P(pole, None, grid, None),
            P(pole, None, None, grid),
            P(grid, None),
            P(pole, None, None, grid),
            P(pole, None),
            P(None, grid),
            P(None, grid),
            P(),
        ),
        out_specs=(
            P(pole, None, None, grid),
            P(pole, None, None, grid),
            P(grid),
            P(grid),
        ),
        check_vma=False,
    )
```

```python
import jax
import jax.numpy as jnp
from jax import lax
from jax.experimental import pallas as pl
from jax.experimental.pallas import tpu as pltpu
from jax.sharding import PartitionSpec as P

F32 = jnp.float32
BF16 = jnp.bfloat16
I32 = jnp.int32
NX, NY, NZ = 4, 2, 8
GROUPS = NX * NY * NZ
POLES = 4
CAP = 8
SLOTS = GROUPS * CAP
PLANE = NY * NZ
COLS = 256
ANC = 1024
ROWS = 1280
QUARTER = ROWS // POLES
SHARD = ANC // GROUPS
MIB = 1024 * 1024
SMEM_SPEC = pl.BlockSpec(memory_space=pltpu.SMEM)
VMEM_SPEC = pl.BlockSpec(memory_space=pltpu.VMEM)
HBM_SPEC = pl.BlockSpec(memory_space=pltpu.HBM)


def params(mib=16):
    return pltpu.CompilerParams(vmem_limit_bytes=mib * MIB)


def mm(a, b, contract=((1,), (0,))):
    return lax.dot_general(a, b, (contract, ((), ())), preferred_element_type=F32)


def iota(shape, dim):
    return lax.broadcasted_iota(I32, shape, dim)


def flag(condition):
    return jnp.where(condition, 1.0, 0.0).astype(BF16)


def split_matmul(values, onehot, contract):
    high = values.astype(BF16)
    rest = values - high.astype(F32)
    middle = rest.astype(BF16)
    low = (rest - middle.astype(F32)).astype(BF16)
    return mm(high, onehot, contract) + mm(middle, onehot, contract) + mm(low, onehot, contract)


def pack_kernel(index, dft, margin, hamiltonian, out0, out1, out2, out3, slot_onehot, both, sems):
    start = pl.multiple_of(index[0] * QUARTER, QUARTER)
    copies = [
        pltpu.make_async_copy(ref.at[pl.ds(start, QUARTER), :], both.at[pl.ds(n * QUARTER, QUARTER), :], sems.at[n])
        for n, ref in enumerate((margin, hamiltonian))
    ]
    for copy in copies:
        copy.start()
    entries = dft[...]
    side = entries.shape[0]
    hit = (entries >> 8) == index[1]
    row, col = iota((side, side), 0), iota((side, side), 1)
    hit_flag = flag(hit)
    rank = mm(hit_flag, flag(row < col))
    previous = mm(flag(((row & 1) == 1) & (col == row - 1)), hit_flag).astype(BF16)
    rank = rank + mm(previous, jnp.ones((side, side), BF16))
    place = ((entries & 255) + 1).astype(F32)
    pair = flag((iota((GROUPS, side), 1) >> 1) == iota((GROUPS, side), 0))
    target = (iota((GROUPS, COLS), 1) + 1).astype(F32)
    pieces = []
    for r in range(CAP):
        picked = jnp.where(hit & (rank == float(r)), place, 0.0).astype(BF16)
        local = jnp.sum(mm(pair, picked), axis=1, keepdims=True)
        pieces.append(flag(local == target))
    by_rank = jnp.concatenate(pieces, axis=0)
    s, t = iota((SLOTS, SLOTS), 0), iota((SLOTS, SLOTS), 1)
    order = flag((s & (CAP - 1)) * GROUPS + (s >> 3) == t)
    slot_onehot[...] = mm(order, by_rank).astype(BF16)
    for copy in copies:
        copy.wait()
    rows = both[...]
    x = index[1] >> 4
    for turn, out in enumerate((out0, out1, out2, out3)):
        first = pl.multiple_of(((x + turn) & (NX - 1)) * (PLANE * CAP), PLANE * CAP)
        out[...] = mm(slot_onehot[pl.ds(first, PLANE * CAP), :], rows, ((1,), (1,))).astype(BF16)


def pack(index, dft, margin, hamiltonian):
    return pl.pallas_call(
        pack_kernel,
        in_specs=[SMEM_SPEC, VMEM_SPEC, HBM_SPEC, HBM_SPEC],
        out_specs=[VMEM_SPEC] * (NX + 1),
        out_shape=[jax.ShapeDtypeStruct((PLANE * CAP, 2 * QUARTER), BF16)] * NX
        + [jax.ShapeDtypeStruct((SLOTS, COLS), BF16)],
        scratch_shapes=[pltpu.VMEM((2 * QUARTER, COLS), BF16), pltpu.SemaphoreType.DMA((2,))],
        compiler_params=params(62),
        name="pack",
    )(index, dft, margin, hamiltonian)


def unpack_kernel(index, dft, arrived, out, column_onehot):
    grid = index[1]
    group_row = jnp.concatenate([dft[pl.ds(2 * grid, 1), :], dft[pl.ds(2 * grid + 1, 1), :]], axis=1) >> 8
    above, across = iota((COLS, COLS), 0), iota((COLS, COLS), 1)
    group_col = jnp.sum(jnp.where(above == across, group_row, 0), axis=1, keepdims=True)
    rank = jnp.sum(jnp.where((group_col == group_row) & (above < across), 1, 0), axis=0, keepdims=True)
    place = iota((SLOTS, COLS), 0)
    column_onehot[...] = flag(place == group_row * CAP + rank)
    turn = ((grid >> 4) - (group_row >> 4)) & (NX - 1)
    slot = (group_row & (PLANE - 1)) * (NX * CAP) + turn * CAP + rank
    out[...] = mm(arrived[...], flag(place == slot), ((0,), (0,))).astype(BF16)


def unpack(index, dft, arrived):
    return pl.pallas_call(
        unpack_kernel,
        in_specs=[SMEM_SPEC] + [VMEM_SPEC] * 2,
        out_specs=[VMEM_SPEC] * 2,
        out_shape=[
            jax.ShapeDtypeStruct((2 * QUARTER, COLS), BF16),
            jax.ShapeDtypeStruct((SLOTS, COLS), BF16),
        ],
        compiler_params=params(),
        name="unpack",
    )(index, dft, arrived)


def upper_kernel(index, fill, lower, *refs):
    early, far_y, second, second_y, far_x, (out, both) = refs[:4], refs[4], refs[5], refs[6], refs[7:10], refs[10:]
    grid = index[1]
    x, y, z = grid >> 4, (grid >> 3) & 1, grid & 7
    for block in range(ANC // COLS):
        keep = fill[0, block].astype(F32).astype(BF16)
        span = slice(block * COLS, (block + 1) * COLS)
        for part in range(2):
            both[span, part * COLS : (part + 1) * COLS] = lower[part, span, :] * keep

    def scatter(refs, places):
        rhs = both[...]
        left, right = [
            mm(jnp.concatenate([ref[:, part].reshape(-1, ANC) for ref in refs], axis=0), rhs) for part in range(2)
        ]
        for n, (dx, dy, dz) in enumerate(places):
            px, py, pz = (x - dx) & (NX - 1), (y - dy) & (NY - 1), (z - dz) & (NZ - 1)
            here = pl.ds(pl.multiple_of(((px * NY + py) * NZ + pz) * SHARD, SHARD), SHARD)
            keep = fill[0, px].astype(F32)
            span = slice(n * SHARD, (n + 1) * SHARD)
            out[0, here, :] = ((right[span, COLS:] - left[span, :COLS]) * keep).astype(BF16)
            out[1, here, :] = ((-left[span, COLS:] - right[span, :COLS]) * keep).astype(BF16)

    up, down = (0, 4, 1, 5), (7, 3, 2, 6)
    scatter(early, [(dx, 0, dz) for dx in range(NX) for dz in up])
    scatter([far_y], [(dx, 1, dz) for dx in range(NX) for dz in up])
    scatter([second, second_y, far_x[0]], [(dx, dy, dz) for dx in range(2) for dy in range(NY) for dz in down])
    scatter(far_x[1:], [(dx, dy, dz) for dx in (2, 3) for dy in range(NY) for dz in down])


def upper_rows(index, fill, lower, pieces):
    return pl.pallas_call(
        upper_kernel,
        in_specs=[SMEM_SPEC] * 2 + [VMEM_SPEC] * (1 + len(pieces)),
        out_specs=VMEM_SPEC,
        out_shape=jax.ShapeDtypeStruct((2, ANC, COLS), BF16),
        scratch_shapes=[pltpu.VMEM((ANC, 2 * COLS), BF16)],
        compiler_params=params(28),
        name="upper",
    )(index, fill, lower, *pieces)


def charge_kernel(index, weights, fill, lower, diag_inverse, own, own_far, mate, mate_far, upper, onehot, slots, rows):
    pole, x = index[0], index[1] >> 4
    for bits, ref in ((0, own), (2, own_far), (1, mate), (3, mate_far)):
        start = pl.multiple_of((pole ^ bits) * QUARTER, QUARTER)
        for which in range(2):
            rows[which, pl.ds(start, QUARTER), :] = ref[which * QUARTER : (which + 1) * QUARTER, :]
    real, imag = weights[0, 0], weights[0, 1]
    sums = real * diag_inverse[1].astype(F32) + imag * diag_inverse[0].astype(F32)
    nears = [rows[which, 0:COLS, :] for which in range(2)]
    totals = [jnp.sum(sums * near.astype(F32), axis=0, keepdims=True) for near in nears]
    both = jnp.concatenate(nears, axis=1)
    for block in range(ANC // COLS):
        keep = fill[0, block].astype(F32)
        span = slice(block * COLS, (block + 1) * COLS)
        up_real, up_imag = upper[0, span, :].astype(F32), upper[1, span, :].astype(F32)
        to_direct = imag * up_real + real * up_imag
        to_cross = imag * up_imag - real * up_real
        direct = mm(lower[0, span, :], both) * keep
        cross = mm(lower[1, span, :], both) * keep
        for which in range(2):
            part = slice(which * COLS, (which + 1) * COLS)
            far = rows[which, (block + 1) * COLS : (block + 2) * COLS, :].astype(F32)
            term = to_direct * (far - direct[:, part]) + to_cross * cross[:, part]
            totals[which] = totals[which] + jnp.sum(term, axis=0, keepdims=True)
    line = iota((8, COLS), 0)
    values = jnp.where(line == 2 * x, totals[0], jnp.where(line == 2 * x + 1, totals[1], 0.0))
    result = split_matmul(values, onehot[...], ((1,), (1,)))
    width = PLANE * CAP
    for px in range(NX):
        for n in range(POLES):
            slots[n * NX + px] = result[:, px * width : (px + 1) * width]


def charge_slots(index, weights, fill, lower, diag_inverse, quarters, upper, onehot):
    return pl.pallas_call(
        charge_kernel,
        in_specs=[SMEM_SPEC] * 3 + [VMEM_SPEC] * (4 + len(quarters)),
        out_specs=VMEM_SPEC,
        out_shape=jax.ShapeDtypeStruct((POLES * NX, 8, PLANE * CAP), F32),
        scratch_shapes=[pltpu.VMEM((2, ROWS, COLS), BF16)],
        compiler_params=params(24),
        name="charge",
    )(index, weights, fill, lower, diag_inverse, *quarters, upper, onehot)


def diag_kernel(fill, lower, upper, diag_inverse, out):
    real = diag_inverse[0].astype(F32)
    imag = diag_inverse[1].astype(F32)
    turn = ((0,), (0,))
    for block in range(ANC // COLS):
        keep = fill[0, block].astype(F32).astype(BF16)
        span = slice(block * COLS, (block + 1) * COLS)
        low_real, low_imag = lower[0, span, :] * keep, lower[1, span, :] * keep
        up_real, up_imag = upper[0, span, :], upper[1, span, :]
        real = real - mm(low_real, up_real, turn) + mm(low_imag, up_imag, turn)
        imag = imag - mm(low_real, up_imag, turn) - mm(low_imag, up_real, turn)
    out[0] = real.astype(BF16)
    out[1] = imag.astype(BF16)


def diag_block(fill, lower, upper, diag_inverse):
    return pl.pallas_call(
        diag_kernel,
        in_specs=[SMEM_SPEC] + [VMEM_SPEC] * 3,
        out_specs=VMEM_SPEC,
        out_shape=jax.ShapeDtypeStruct((2, COLS, COLS), BF16),
        compiler_params=params(),
        name="diag",
    )(fill, lower, upper, diag_inverse)


def turn_kernel(arrived, out):
    total = jnp.sum(arrived[...], axis=0)
    width = PLANE * CAP
    for n in range(PLANE):
        out[n] = total if n == 0 else pltpu.roll(total, width - n * CAP, 1)


def turn(arrived):
    return pl.pallas_call(
        turn_kernel,
        in_specs=[VMEM_SPEC],
        out_specs=VMEM_SPEC,
        out_shape=jax.ShapeDtypeStruct((PLANE, 8, PLANE * CAP), F32),
        compiler_params=params(),
        name="turn",
    )(arrived)


def place_kernel(arrived, onehot, *outs):
    width = PLANE * CAP
    line, lane = iota((8, width), 0), iota((8, width), 1)
    total = jnp.zeros((8, width), F32)
    for n in range(PLANE):
        piece = jnp.where(lane < CAP, arrived[n], 0.0)
        total = total + (piece if n == 0 else pltpu.roll(piece, n * CAP, 1))
    wide = jnp.concatenate([jnp.where((line >> 1) == px, total, 0.0) for px in range(NX)], axis=1)
    result = split_matmul(wide, onehot[...], ((1,), (0,)))
    for which in range(2):
        outs[which][...] = jnp.sum(
            jnp.where((iota((8, COLS), 0) & 1) == which, result, 0.0), axis=0, keepdims=True
        )


def place(arrived, onehot):
    return pl.pallas_call(
        place_kernel,
        in_specs=[VMEM_SPEC] * 2,
        out_specs=[VMEM_SPEC] * 2,
        out_shape=[jax.ShapeDtypeStruct((1, COLS), F32)] * 2,
        compiler_params=params(),
        name="place",
    )(arrived, onehot)


SIZES = {"ylo": 2, "core": 2, "x": NX, "yhi": NY, "z": NZ}


def shift(value, axis, by):
    size = SIZES[axis]
    return lax.ppermute(value, axis, [(n, (n + by) % size) for n in range(size)])


def all_of_z(value):
    pair = jnp.stack([value, shift(value, "z", 4)])
    return [pair, shift(pair, "z", 1), shift(pair, "z", -1), shift(pair, "z", 2)]


def body(ainv_anc, lower_panels, fill_pattern, diag_inverse, pole_weights, hamiltonian, margin, dft_column):
    pole = lax.axis_index("ylo") * 2 + lax.axis_index("core")
    grid = (lax.axis_index("x") * NY + lax.axis_index("yhi")) * NZ + lax.axis_index("z")
    index = jnp.stack([pole, grid]).astype(I32)
    lower, inverse = lower_panels[0], diag_inverse[0]
    shard = ainv_anc[0]

    table = dft_column.reshape(128, 128)
    z_4 = shift(shard, "z", 4)
    *packed, slot_onehot = pack(index, table, margin, hamiltonian)
    z_4, *packed = lax.optimization_barrier((z_4, *packed))

    near = jnp.stack([shard, z_4])
    near_up, near_down, near_two = [shift(near, "z", d) for d in (1, -1, 2)]
    packed = [value.reshape(PLANE, CAP, 2 * QUARTER) for value in packed]
    sent = [packed[0]] + [shift(packed[d], "x", d) for d in (1, 2, 3)]
    near, near_up, near_down, near_two, *sent = lax.optimization_barrier((near, near_up, near_down, near_two, *sent))

    first = jnp.concatenate([near, near_up])
    second = jnp.concatenate([near_down, near_two])
    first_x = [first] + [shift(first, "x", d) for d in (1, 2, 3)]
    second_y = [second, shift(second, "yhi", 1)]
    arrived = lax.all_to_all(jnp.stack(sent, axis=1), ("yhi", "z"), split_axis=0, concat_axis=0, tiled=True)
    (first_x, second_y, arrived) = lax.optimization_barrier((first_x, second_y, arrived))

    first_y = shift(jnp.concatenate(first_x), "yhi", 1)
    second_all = jnp.concatenate(second_y)
    second_x = [shift(second_all, "x", d) for d in (1, 2, 3)]
    mine, column_onehot = unpack(index, table, arrived.reshape(SLOTS, 2 * QUARTER))
    mine_far = shift(mine, "ylo", 1)
    (first_y, second_x, mine_far) = lax.optimization_barrier((first_y, second_x, mine_far))

    mates = shift(jnp.stack([mine, mine_far]), "core", 1)
    mate, mate_far = mates[0], mates[1]
    upper = upper_rows(index, fill_pattern, lower, first_x + [first_y] + second_y + second_x)
    quarters = [mine, mine_far, mate, mate_far]
    slots = charge_slots(index, pole_weights, fill_pattern, lower, inverse, quarters, upper, column_onehot)
    diag = diag_block(fill_pattern, lower, upper, inverse)
    sums = lax.all_to_all(slots, ("ylo", "core", "x"), split_axis=0, concat_axis=0, tiled=True)
    sums = lax.all_to_all(turn(sums), ("yhi", "z"), split_axis=0, concat_axis=0, tiled=True)
    charges, energy = place(sums, slot_onehot)
    return (upper[None], diag[None], charges.reshape(COLS), energy.reshape(COLS))


def solution(mesh):
    fine = jax.sharding.Mesh(mesh.devices.reshape(2, 2, NX, NY, NZ), ("ylo", "core", "x", "yhi", "z"))
    pole, grid = ("ylo", "core"), ("x", "yhi", "z")
    return jax.shard_map(
        body,
        mesh=fine,
        in_specs=(
            P(pole, None, grid, None),
            P(pole, None, None, grid),
            P(grid, None),
            P(pole, None, None, grid),
            P(pole, None),
            P(None, grid),
            P(None, grid),
            P(),
        ),
        out_specs=(
            P(pole, None, None, grid),
            P(pole, None, None, grid),
            P(grid),
            P(grid),
        ),
        check_vma=False,
    )
```

```python
import jax
import jax.numpy as jnp
from jax import lax
from jax.experimental import pallas as pl
from jax.experimental.pallas import tpu as pltpu
from jax.sharding import PartitionSpec as P

F32 = jnp.float32
BF16 = jnp.bfloat16
I32 = jnp.int32
NX, NY, NZ = 4, 2, 8
GROUPS = NX * NY * NZ
POLES = 4
CAP = 8
SLOTS = GROUPS * CAP
PLANE = NY * NZ
COLS = 256
ANC = 1024
ROWS = 1280
QUARTER = ROWS // POLES
SHARD = ANC // GROUPS
MIB = 1024 * 1024
SMEM_SPEC = pl.BlockSpec(memory_space=pltpu.SMEM)
VMEM_SPEC = pl.BlockSpec(memory_space=pltpu.VMEM)
HBM_SPEC = pl.BlockSpec(memory_space=pltpu.HBM)


def params(mib=16):
    return pltpu.CompilerParams(vmem_limit_bytes=mib * MIB)


def mm(a, b, contract=((1,), (0,))):
    return lax.dot_general(a, b, (contract, ((), ())), preferred_element_type=F32)


def iota(shape, dim):
    return lax.broadcasted_iota(I32, shape, dim)


def flag(condition):
    return jnp.where(condition, 1.0, 0.0).astype(BF16)


def split_matmul(values, onehot, contract):
    high = values.astype(BF16)
    rest = values - high.astype(F32)
    middle = rest.astype(BF16)
    low = (rest - middle.astype(F32)).astype(BF16)
    return mm(high, onehot, contract) + mm(middle, onehot, contract) + mm(low, onehot, contract)


def pack_kernel(index, dft, margin, hamiltonian, out0, out1, out2, out3, slot_onehot, both, sems):
    start = pl.multiple_of(index[0] * QUARTER, QUARTER)
    copies = [
        pltpu.make_async_copy(ref.at[pl.ds(start, QUARTER), :], both.at[pl.ds(n * QUARTER, QUARTER), :], sems.at[n])
        for n, ref in enumerate((margin, hamiltonian))
    ]
    for copy in copies:
        copy.start()
    entries = dft[...]
    side = entries.shape[0]
    hit = (entries >> 8) == index[1]
    row, col = iota((side, side), 0), iota((side, side), 1)
    hit_flag = flag(hit)
    rank = mm(hit_flag, flag(row < col))
    previous = mm(flag(((row & 1) == 1) & (col == row - 1)), hit_flag).astype(BF16)
    rank = rank + mm(previous, jnp.ones((side, side), BF16))
    place = ((entries & 255) + 1).astype(F32)
    pair = flag((iota((GROUPS, side), 1) >> 1) == iota((GROUPS, side), 0))
    target = (iota((GROUPS, COLS), 1) + 1).astype(F32)
    pieces = []
    for r in range(CAP):
        picked = jnp.where(hit & (rank == float(r)), place, 0.0).astype(BF16)
        local = jnp.sum(mm(pair, picked), axis=1, keepdims=True)
        pieces.append(flag(local == target))
    by_rank = jnp.concatenate(pieces, axis=0)
    s, t = iota((SLOTS, SLOTS), 0), iota((SLOTS, SLOTS), 1)
    order = flag((s & (CAP - 1)) * GROUPS + (s >> 3) == t)
    slot_onehot[...] = mm(order, by_rank).astype(BF16)
    for copy in copies:
        copy.wait()
    rows = both[...]
    x = index[1] >> 4
    for turn, out in enumerate((out0, out1, out2, out3)):
        first = pl.multiple_of(((x + turn) & (NX - 1)) * (PLANE * CAP), PLANE * CAP)
        out[...] = mm(slot_onehot[pl.ds(first, PLANE * CAP), :], rows, ((1,), (1,))).astype(BF16)


def pack(index, dft, margin, hamiltonian):
    return pl.pallas_call(
        pack_kernel,
        in_specs=[SMEM_SPEC, VMEM_SPEC, HBM_SPEC, HBM_SPEC],
        out_specs=[VMEM_SPEC] * (NX + 1),
        out_shape=[jax.ShapeDtypeStruct((PLANE * CAP, 2 * QUARTER), BF16)] * NX
        + [jax.ShapeDtypeStruct((SLOTS, COLS), BF16)],
        scratch_shapes=[pltpu.VMEM((2 * QUARTER, COLS), BF16), pltpu.SemaphoreType.DMA((2,))],
        compiler_params=params(62),
        name="pack",
    )(index, dft, margin, hamiltonian)


def unpack_kernel(index, dft, arrived, out, column_onehot):
    grid = index[1]
    group_row = jnp.concatenate([dft[pl.ds(2 * grid, 1), :], dft[pl.ds(2 * grid + 1, 1), :]], axis=1) >> 8
    above, across = iota((COLS, COLS), 0), iota((COLS, COLS), 1)
    group_col = jnp.sum(jnp.where(above == across, group_row, 0), axis=1, keepdims=True)
    rank = jnp.sum(jnp.where((group_col == group_row) & (above < across), 1, 0), axis=0, keepdims=True)
    place = iota((SLOTS, COLS), 0)
    column_onehot[...] = flag(place == group_row * CAP + rank)
    turn = ((grid >> 4) - (group_row >> 4)) & (NX - 1)
    slot = (group_row & (PLANE - 1)) * (NX * CAP) + turn * CAP + rank
    out[...] = mm(arrived[...], flag(place == slot), ((0,), (0,))).astype(BF16)


def unpack(index, dft, arrived):
    return pl.pallas_call(
        unpack_kernel,
        in_specs=[SMEM_SPEC] + [VMEM_SPEC] * 2,
        out_specs=[VMEM_SPEC] * 2,
        out_shape=[
            jax.ShapeDtypeStruct((2 * QUARTER, COLS), BF16),
            jax.ShapeDtypeStruct((SLOTS, COLS), BF16),
        ],
        compiler_params=params(),
        name="unpack",
    )(index, dft, arrived)


UP, DOWN = (0, 4, 1, 5), (7, 3, 2, 6)


def product(refs, rhs):
    left, right = [
        mm(jnp.concatenate([ref[:, part].reshape(-1, ANC) for ref in refs], axis=0), rhs[...]) for part in range(2)
    ]
    return right[:, COLS:] - left[:, :COLS], -left[:, COLS:] - right[:, :COLS]


def start_kernel(fill, lower, *refs):
    first, second, (rhs, out) = refs[:4], refs[4:6], refs[6:]
    for block in range(ANC // COLS):
        keep = fill[0, block].astype(F32).astype(BF16)
        span = slice(block * COLS, (block + 1) * COLS)
        for part in range(2):
            rhs[span, part * COLS : (part + 1) * COLS] = lower[part, span, :] * keep
    rows = 0
    for group in (first, second):
        real, imag = product(group, rhs)
        span = slice(rows, rows + real.shape[0])
        out[0, span, :] = real.astype(BF16)
        out[1, span, :] = imag.astype(BF16)
        rows = rows + real.shape[0]


def start_rows(fill, lower, pieces):
    rows = sum(value.shape[0] for value in pieces) * SHARD
    return pl.pallas_call(
        start_kernel,
        in_specs=[SMEM_SPEC] + [VMEM_SPEC] * (1 + len(pieces)),
        out_specs=[VMEM_SPEC] * 2,
        out_shape=[
            jax.ShapeDtypeStruct((ANC, 2 * COLS), BF16),
            jax.ShapeDtypeStruct((2, rows, COLS), BF16),
        ],
        compiler_params=params(16),
        name="start",
    )(fill, lower, *pieces)


def upper_kernel(index, fill, rhs, early, first_y, second_1, second_2, second_3, *outs):
    grid = index[1]
    x, y, z = grid >> 4, (grid >> 3) & 1, grid & 7

    def scatter(real, imag, places):
        for n, (dx, dy, dz) in enumerate(places):
            px, py, pz = (x - dx) & (NX - 1), (y - dy) & (NY - 1), (z - dz) & (NZ - 1)
            here = pl.ds(pl.multiple_of(((px * NY + py) * NZ + pz) * SHARD, SHARD), SHARD)
            keep = fill[0, px].astype(F32)
            span = slice(n * SHARD, (n + 1) * SHARD)
            for part, value in enumerate((real, imag)):
                rows = (value[span].astype(F32) * keep).astype(BF16)
                for out in outs:
                    out[part, here, :] = rows

    def places(dxs, dys, dzs):
        return [(dx, dy, dz) for dx in dxs for dy in dys for dz in dzs]

    scatter(early[0], early[1], places(range(NX), (0,), UP) + places((0,), range(NY), DOWN))
    real, imag = product([first_y], rhs)
    scatter(real, imag, places(range(NX), (1,), UP))
    real, imag = product([second_1, second_2, second_3], rhs)
    scatter(real, imag, places((1, 2, 3), range(NY), DOWN))


def upper_rows(index, fill, rhs, early, pieces):
    shape = jax.ShapeDtypeStruct((2, ANC, COLS), BF16)
    return pl.pallas_call(
        upper_kernel,
        in_specs=[SMEM_SPEC] * 2 + [VMEM_SPEC] * (2 + len(pieces)),
        out_specs=[VMEM_SPEC] * 2,
        out_shape=[shape, shape],
        compiler_params=params(20),
        name="upper",
    )(index, fill, rhs, early, *pieces)


def charge_kernel(index, weights, fill, lower, diag_inverse, own, own_far, mate, mate_far, upper, onehot, slots, rows):
    pole, x = index[0], index[1] >> 4
    for bits, ref in ((0, own), (2, own_far), (1, mate), (3, mate_far)):
        start = pl.multiple_of((pole ^ bits) * QUARTER, QUARTER)
        for which in range(2):
            rows[which, pl.ds(start, QUARTER), :] = ref[which * QUARTER : (which + 1) * QUARTER, :]
    real, imag = weights[0, 0], weights[0, 1]
    sums = real * diag_inverse[1].astype(F32) + imag * diag_inverse[0].astype(F32)
    nears = [rows[which, 0:COLS, :] for which in range(2)]
    totals = [jnp.sum(sums * near.astype(F32), axis=0, keepdims=True) for near in nears]
    both = jnp.concatenate(nears, axis=1)
    for block in range(ANC // COLS):
        keep = fill[0, block].astype(F32)
        span = slice(block * COLS, (block + 1) * COLS)
        up_real, up_imag = upper[0, span, :].astype(F32), upper[1, span, :].astype(F32)
        to_direct = imag * up_real + real * up_imag
        to_cross = imag * up_imag - real * up_real
        direct = mm(lower[0, span, :], both) * keep
        cross = mm(lower[1, span, :], both) * keep
        for which in range(2):
            part = slice(which * COLS, (which + 1) * COLS)
            far = rows[which, (block + 1) * COLS : (block + 2) * COLS, :].astype(F32)
            term = to_direct * (far - direct[:, part]) + to_cross * cross[:, part]
            totals[which] = totals[which] + jnp.sum(term, axis=0, keepdims=True)
    line = iota((8, COLS), 0)
    values = jnp.where(line == 2 * x, totals[0], jnp.where(line == 2 * x + 1, totals[1], 0.0))
    result = split_matmul(values, onehot[...], ((1,), (1,)))
    width = PLANE * CAP
    for px in range(NX):
        for n in range(POLES):
            slots[n * NX + px] = result[:, px * width : (px + 1) * width]


def charge_slots(index, weights, fill, lower, diag_inverse, quarters, upper, onehot):
    return pl.pallas_call(
        charge_kernel,
        in_specs=[SMEM_SPEC] * 3 + [VMEM_SPEC] * (4 + len(quarters)),
        out_specs=VMEM_SPEC,
        out_shape=jax.ShapeDtypeStruct((POLES * NX, 8, PLANE * CAP), F32),
        scratch_shapes=[pltpu.VMEM((2, ROWS, COLS), BF16)],
        compiler_params=params(24),
        name="charge",
    )(index, weights, fill, lower, diag_inverse, *quarters, upper, onehot)


def diag_kernel(fill, lower, upper, diag_inverse, out):
    real = diag_inverse[0].astype(F32)
    imag = diag_inverse[1].astype(F32)
    turn = ((0,), (0,))
    for block in range(ANC // COLS):
        keep = fill[0, block].astype(F32).astype(BF16)
        span = slice(block * COLS, (block + 1) * COLS)
        low_real, low_imag = lower[0, span, :] * keep, lower[1, span, :] * keep
        up_real, up_imag = upper[0, span, :], upper[1, span, :]
        real = real - mm(low_real, up_real, turn) + mm(low_imag, up_imag, turn)
        imag = imag - mm(low_real, up_imag, turn) - mm(low_imag, up_real, turn)
    out[0] = real.astype(BF16)
    out[1] = imag.astype(BF16)


def diag_block(fill, lower, upper, diag_inverse):
    return pl.pallas_call(
        diag_kernel,
        in_specs=[SMEM_SPEC] + [VMEM_SPEC] * 3,
        out_specs=VMEM_SPEC,
        out_shape=jax.ShapeDtypeStruct((2, COLS, COLS), BF16),
        compiler_params=params(),
        name="diag",
    )(fill, lower, upper, diag_inverse)


def turn_kernel(arrived, out):
    total = jnp.sum(arrived[...], axis=0)
    width = PLANE * CAP
    for n in range(PLANE):
        out[n] = total if n == 0 else pltpu.roll(total, width - n * CAP, 1)


def turn(arrived):
    return pl.pallas_call(
        turn_kernel,
        in_specs=[VMEM_SPEC],
        out_specs=VMEM_SPEC,
        out_shape=jax.ShapeDtypeStruct((PLANE, 8, PLANE * CAP), F32),
        compiler_params=params(),
        name="turn",
    )(arrived)


def place_kernel(arrived, onehot, *outs):
    width = PLANE * CAP
    line, lane = iota((8, width), 0), iota((8, width), 1)
    total = jnp.zeros((8, width), F32)
    for n in range(PLANE):
        piece = jnp.where(lane < CAP, arrived[n], 0.0)
        total = total + (piece if n == 0 else pltpu.roll(piece, n * CAP, 1))
    wide = jnp.concatenate([jnp.where((line >> 1) == px, total, 0.0) for px in range(NX)], axis=1)
    result = split_matmul(wide, onehot[...], ((1,), (0,)))
    for which in range(2):
        outs[which][...] = jnp.sum(
            jnp.where((iota((8, COLS), 0) & 1) == which, result, 0.0), axis=0, keepdims=True
        )


def place(arrived, onehot):
    return pl.pallas_call(
        place_kernel,
        in_specs=[VMEM_SPEC] * 2,
        out_specs=[VMEM_SPEC] * 2,
        out_shape=[jax.ShapeDtypeStruct((1, COLS), F32)] * 2,
        compiler_params=params(),
        name="place",
    )(arrived, onehot)


SIZES = {"ylo": 2, "core": 2, "x": NX, "yhi": NY, "z": NZ}


def shift(value, axis, by):
    size = SIZES[axis]
    return lax.ppermute(value, axis, [(n, (n + by) % size) for n in range(size)])


def all_of_z(value):
    pair = jnp.stack([value, shift(value, "z", 4)])
    return [pair, shift(pair, "z", 1), shift(pair, "z", -1), shift(pair, "z", 2)]


def body(ainv_anc, lower_panels, fill_pattern, diag_inverse, pole_weights, hamiltonian, margin, dft_column):
    pole = lax.axis_index("ylo") * 2 + lax.axis_index("core")
    grid = (lax.axis_index("x") * NY + lax.axis_index("yhi")) * NZ + lax.axis_index("z")
    index = jnp.stack([pole, grid]).astype(I32)
    lower, inverse = lower_panels[0], diag_inverse[0]
    shard = ainv_anc[0]

    table = dft_column.reshape(128, 128)
    *packed, slot_onehot = pack(index, table, margin, hamiltonian)
    z_4 = shift(shard, "z", 4)
    z_4, *packed = lax.optimization_barrier((z_4, *packed))

    near = jnp.stack([shard, z_4])
    packed = [value.reshape(PLANE, CAP, 2 * QUARTER) for value in packed]
    sent = [packed[0]] + [shift(packed[d], "x", d) for d in (1, 2, 3)]
    near_up, near_down, near_two = [shift(near, "z", d) for d in (1, -1, 2)]
    near, near_up, near_down, near_two, *sent = lax.optimization_barrier((near, near_up, near_down, near_two, *sent))

    first = jnp.concatenate([near, near_up])
    second = jnp.concatenate([near_down, near_two])
    first_x = [first] + [shift(first, "x", d) for d in (1, 2, 3)]
    second_y = [second, shift(second, "yhi", 1)]
    arrived = lax.all_to_all(jnp.stack(sent, axis=1), ("yhi", "z"), split_axis=0, concat_axis=0, tiled=True)
    (first_x, second_y, arrived) = lax.optimization_barrier((first_x, second_y, arrived))

    first_y = shift(jnp.concatenate(first_x), "yhi", 1)
    second_all = jnp.concatenate(second_y)
    second_x = [shift(second_all, "x", d) for d in (1, 2, 3)]
    mine, column_onehot = unpack(index, table, arrived.reshape(SLOTS, 2 * QUARTER))
    mine_far = shift(mine, "ylo", 1)
    rhs, early = start_rows(fill_pattern, lower, first_x + second_y)
    first_y, second_x, mine_far, early = lax.optimization_barrier((first_y, second_x, mine_far, early))

    mates = shift(jnp.stack([mine, mine_far]), "core", 1)
    mate, mate_far = mates[0], mates[1]
    upper, upper_again = upper_rows(index, fill_pattern, rhs, early, [first_y] + second_x)
    quarters = [mine, mine_far, mate, mate_far]
    slots = charge_slots(index, pole_weights, fill_pattern, lower, inverse, quarters, upper_again, column_onehot)
    diag = diag_block(fill_pattern, lower, upper_again, inverse)
    sums = lax.all_to_all(slots, ("ylo", "core", "x"), split_axis=0, concat_axis=0, tiled=True)
    sums = lax.all_to_all(turn(sums), ("yhi", "z"), split_axis=0, concat_axis=0, tiled=True)
    charges, energy = place(sums, slot_onehot)
    return (upper[None], diag[None], charges.reshape(COLS), energy.reshape(COLS))


def solution(mesh):
    fine = jax.sharding.Mesh(mesh.devices.reshape(2, 2, NX, NY, NZ), ("ylo", "core", "x", "yhi", "z"))
    pole, grid = ("ylo", "core"), ("x", "yhi", "z")
    return jax.shard_map(
        body,
        mesh=fine,
        in_specs=(
            P(pole, None, grid, None),
            P(pole, None, None, grid),
            P(grid, None),
            P(pole, None, None, grid),
            P(pole, None),
            P(None, grid),
            P(None, grid),
            P(),
        ),
        out_specs=(
            P(pole, None, None, grid),
            P(pole, None, None, grid),
            P(grid),
            P(grid),
        ),
        check_vma=False,
    )
```

```python
import jax
import jax.numpy as jnp
from jax import lax
from jax.experimental import pallas as pl
from jax.experimental.pallas import tpu as pltpu
from jax.sharding import PartitionSpec as P

F32 = jnp.float32
BF16 = jnp.bfloat16
I32 = jnp.int32
NX, NY, NZ = 4, 2, 8
GROUPS = NX * NY * NZ
POLES = 4
CAP = 8
SLOTS = GROUPS * CAP
PLANE = NY * NZ
COLS = 256
ANC = 1024
ROWS = 1280
QUARTER = ROWS // POLES
SHARD = ANC // GROUPS
PART = 896
MIB = 1024 * 1024
SMEM_SPEC = pl.BlockSpec(memory_space=pltpu.SMEM)
VMEM_SPEC = pl.BlockSpec(memory_space=pltpu.VMEM)
HBM_SPEC = pl.BlockSpec(memory_space=pltpu.HBM)


def params(mib=16):
    return pltpu.CompilerParams(vmem_limit_bytes=mib * MIB)


def mm(a, b, contract=((1,), (0,))):
    return lax.dot_general(a, b, (contract, ((), ())), preferred_element_type=F32)


def iota(shape, dim):
    return lax.broadcasted_iota(I32, shape, dim)


def flag(condition):
    return jnp.where(condition, 1.0, 0.0).astype(BF16)


def split_matmul(values, onehot, contract):
    high = values.astype(BF16)
    rest = values - high.astype(F32)
    middle = rest.astype(BF16)
    low = (rest - middle.astype(F32)).astype(BF16)
    return mm(high, onehot, contract) + mm(middle, onehot, contract) + mm(low, onehot, contract)


def pack_kernel(index, dft, margin, hamiltonian, out0, out1, out2, out3, slot_onehot, both, sems):
    start = pl.multiple_of(index[0] * QUARTER, QUARTER)
    copies = [
        pltpu.make_async_copy(ref.at[pl.ds(start, QUARTER), :], both.at[pl.ds(n * QUARTER, QUARTER), :], sems.at[n])
        for n, ref in enumerate((margin, hamiltonian))
    ]
    for copy in copies:
        copy.start()
    entries = dft[...]
    side = entries.shape[0]
    hit = (entries >> 8) == index[1]
    row, col = iota((side, side), 0), iota((side, side), 1)
    hit_flag = flag(hit)
    rank = mm(hit_flag, flag(row < col))
    previous = mm(flag(((row & 1) == 1) & (col == row - 1)), hit_flag).astype(BF16)
    rank = rank + mm(previous, jnp.ones((side, side), BF16))
    place = ((entries & 255) + 1).astype(F32)
    pair = flag((iota((GROUPS, side), 1) >> 1) == iota((GROUPS, side), 0))
    target = (iota((GROUPS, COLS), 1) + 1).astype(F32)
    pieces = []
    for r in range(CAP):
        picked = jnp.where(hit & (rank == float(r)), place, 0.0).astype(BF16)
        local = jnp.sum(mm(pair, picked), axis=1, keepdims=True)
        pieces.append(flag(local == target))
    by_rank = jnp.concatenate(pieces, axis=0)
    s, t = iota((SLOTS, SLOTS), 0), iota((SLOTS, SLOTS), 1)
    order = flag((s & (CAP - 1)) * GROUPS + (s >> 3) == t)
    slot_onehot[...] = mm(order, by_rank).astype(BF16)
    for copy in copies:
        copy.wait()
    rows = both[...]
    x = index[1] >> 4
    for turn, out in enumerate((out0, out1, out2, out3)):
        first = pl.multiple_of(((x + turn) & (NX - 1)) * (PLANE * CAP), PLANE * CAP)
        out[...] = mm(slot_onehot[pl.ds(first, PLANE * CAP), :], rows, ((1,), (1,))).astype(BF16)


def pack(index, dft, margin, hamiltonian):
    return pl.pallas_call(
        pack_kernel,
        in_specs=[SMEM_SPEC, VMEM_SPEC, HBM_SPEC, HBM_SPEC],
        out_specs=[VMEM_SPEC] * (NX + 1),
        out_shape=[jax.ShapeDtypeStruct((PLANE * CAP, 2 * QUARTER), BF16)] * NX
        + [jax.ShapeDtypeStruct((SLOTS, COLS), BF16)],
        scratch_shapes=[pltpu.VMEM((2 * QUARTER, COLS), BF16), pltpu.SemaphoreType.DMA((2,))],
        compiler_params=params(62),
        name="pack",
    )(index, dft, margin, hamiltonian)


def unpack_kernel(index, dft, arrived, out, column_onehot):
    grid = index[1]
    group_row = jnp.concatenate([dft[pl.ds(2 * grid, 1), :], dft[pl.ds(2 * grid + 1, 1), :]], axis=1) >> 8
    above, across = iota((COLS, COLS), 0), iota((COLS, COLS), 1)
    group_col = jnp.sum(jnp.where(above == across, group_row, 0), axis=1, keepdims=True)
    rank = jnp.sum(jnp.where((group_col == group_row) & (above < across), 1, 0), axis=0, keepdims=True)
    place = iota((SLOTS, COLS), 0)
    column_onehot[...] = flag(place == group_row * CAP + rank)
    turn = ((grid >> 4) - (group_row >> 4)) & (NX - 1)
    slot = (group_row & (PLANE - 1)) * (NX * CAP) + turn * CAP + rank
    out[...] = mm(arrived[...], flag(place == slot), ((0,), (0,))).astype(BF16)


def unpack(index, dft, arrived):
    return pl.pallas_call(
        unpack_kernel,
        in_specs=[SMEM_SPEC] + [VMEM_SPEC] * 2,
        out_specs=[VMEM_SPEC] * 2,
        out_shape=[
            jax.ShapeDtypeStruct((2 * QUARTER, COLS), BF16),
            jax.ShapeDtypeStruct((SLOTS, COLS), BF16),
        ],
        compiler_params=params(),
        name="unpack",
    )(index, dft, arrived)


UP, DOWN = (0, 4, 1, 5), (7, 3, 2, 6)


def product(lefts, rhs):
    left, right = [mm(lefts(part), rhs) for part in range(2)]
    return right[:, COLS:] - left[:, :COLS], -left[:, COLS:] - right[:, :COLS]


def rows_of(refs, part, columns):
    return jnp.concatenate([ref[:, part, :, columns].reshape(-1, columns.stop - columns.start) for ref in refs], axis=0)


WHOLE, NEAR, REST = slice(0, ANC), slice(0, PART), slice(ANC, 2 * ANC - PART)


def start_kernel(weights, fill, lower, diag_inverse, *refs):
    first, second, (rhs, out, sums) = refs[:4], refs[4:6], refs[6:]
    for block in range(ANC // COLS):
        keep = fill[0, block].astype(F32).astype(BF16)
        span = slice(block * COLS, (block + 1) * COLS)
        for part in range(2):
            rhs[span, part * COLS : (part + 1) * COLS] = lower[part, span, :] * keep
    sums[...] = weights[0, 0] * diag_inverse[1].astype(F32) + weights[0, 1] * diag_inverse[0].astype(F32)
    rows = 0
    for group, columns in ((first, NEAR), (second, WHOLE)):
        real, imag = product(lambda part: rows_of(group, part, columns), rhs[columns, :])
        span = slice(rows, rows + real.shape[0])
        out[0, span, :] = real
        out[1, span, :] = imag
        rows = rows + real.shape[0]


def start_rows(weights, fill, lower, diag_inverse, pieces):
    rows = sum(value.shape[0] for value in pieces) * SHARD
    return pl.pallas_call(
        start_kernel,
        in_specs=[SMEM_SPEC] * 2 + [VMEM_SPEC] * (2 + len(pieces)),
        out_specs=[VMEM_SPEC] * 3,
        out_shape=[
            jax.ShapeDtypeStruct((ANC, 2 * COLS), BF16),
            jax.ShapeDtypeStruct((2, rows, COLS), F32),
            jax.ShapeDtypeStruct((COLS, COLS), F32),
        ],
        compiler_params=params(16),
        name="start",
    )(weights, fill, lower, diag_inverse, *pieces)


def upper_kernel(index, fill, rhs, early, first_y, second_0, second_y, second_1, second_2, second_3, *outs):
    grid = index[1]
    x, y, z = grid >> 4, (grid >> 3) & 1, grid & 7

    def scatter(real, imag, places):
        for n, (dx, dy, dz) in enumerate(places):
            px, py, pz = (x - dx) & (NX - 1), (y - dy) & (NY - 1), (z - dz) & (NZ - 1)
            here = pl.ds(pl.multiple_of(((px * NY + py) * NZ + pz) * SHARD, SHARD), SHARD)
            keep = fill[0, px].astype(F32)
            span = slice(n * SHARD, (n + 1) * SHARD)
            for part, value in enumerate((real, imag)):
                rows = (value[span] * keep).astype(BF16)
                for out in outs:
                    out[part, here, :] = rows

    def places(dxs, dys, dzs):
        return [(dx, dy, dz) for dx in dxs for dy in dys for dz in dzs]

    far = (second_1, second_2, second_3)
    own = NX * len(UP) * SHARD
    real, imag = product(lambda part: rows_of([second_0] + [ref.at[0:4] for ref in far], part, REST), rhs[PART:ANC, :])
    scatter(real + early[0, 0:own, :], imag + early[1, 0:own, :], places(range(NX), (0,), UP))
    scatter(early[0, own:, :], early[1, own:, :], places((0,), range(NY), DOWN))
    real, imag = product(lambda part: rows_of([second_y] + [ref.at[4:8] for ref in far], part, REST), rhs[PART:ANC, :])
    more_real, more_imag = product(lambda part: rows_of([first_y], part, NEAR), rhs[NEAR, :])
    scatter(real + more_real, imag + more_imag, places(range(NX), (1,), UP))
    real, imag = product(lambda part: rows_of(far, part, WHOLE), rhs[...])
    scatter(real, imag, places((1, 2, 3), range(NY), DOWN))


def upper_rows(index, fill, rhs, early, pieces):
    shape = jax.ShapeDtypeStruct((2, ANC, COLS), BF16)
    return pl.pallas_call(
        upper_kernel,
        in_specs=[SMEM_SPEC] * 2 + [VMEM_SPEC] * (2 + len(pieces)),
        out_specs=[VMEM_SPEC] * 2,
        out_shape=[shape, shape],
        compiler_params=params(20),
        name="upper",
    )(index, fill, rhs, early, *pieces)


def charge_kernel(index, weights, fill, lower, sums, own, own_far, mate, mate_far, upper, onehot, slots, rows):
    pole, x = index[0], index[1] >> 4
    for bits, ref in ((0, own), (2, own_far), (1, mate), (3, mate_far)):
        start = pl.multiple_of((pole ^ bits) * QUARTER, QUARTER)
        for which in range(2):
            rows[which, pl.ds(start, QUARTER), :] = ref[which * QUARTER : (which + 1) * QUARTER, :]
    real, imag = weights[0, 0], weights[0, 1]
    nears = [rows[which, 0:COLS, :] for which in range(2)]
    totals = [jnp.sum(sums[...] * near.astype(F32), axis=0, keepdims=True) for near in nears]
    both = jnp.concatenate(nears, axis=1)
    for block in range(ANC // COLS):
        keep = fill[0, block].astype(F32)
        span = slice(block * COLS, (block + 1) * COLS)
        up_real, up_imag = upper[0, span, :].astype(F32), upper[1, span, :].astype(F32)
        to_direct = imag * up_real + real * up_imag
        to_cross = imag * up_imag - real * up_real
        direct = mm(lower[0, span, :], both) * keep
        cross = mm(lower[1, span, :], both) * keep
        for which in range(2):
            part = slice(which * COLS, (which + 1) * COLS)
            far = rows[which, (block + 1) * COLS : (block + 2) * COLS, :].astype(F32)
            term = to_direct * (far - direct[:, part]) + to_cross * cross[:, part]
            totals[which] = totals[which] + jnp.sum(term, axis=0, keepdims=True)
    line = iota((8, COLS), 0)
    values = jnp.where(line == 2 * x, totals[0], jnp.where(line == 2 * x + 1, totals[1], 0.0))
    result = split_matmul(values, onehot[...], ((1,), (1,)))
    width = PLANE * CAP
    for px in range(NX):
        for n in range(POLES):
            slots[n * NX + px] = result[:, px * width : (px + 1) * width]


def charge_slots(index, weights, fill, lower, sums, quarters, upper, onehot):
    return pl.pallas_call(
        charge_kernel,
        in_specs=[SMEM_SPEC] * 3 + [VMEM_SPEC] * (4 + len(quarters)),
        out_specs=VMEM_SPEC,
        out_shape=jax.ShapeDtypeStruct((POLES * NX, 8, PLANE * CAP), F32),
        scratch_shapes=[pltpu.VMEM((2, ROWS, COLS), BF16)],
        compiler_params=params(24),
        name="charge",
    )(index, weights, fill, lower, sums, *quarters, upper, onehot)


def diag_kernel(fill, lower, upper, diag_inverse, out):
    real = diag_inverse[0].astype(F32)
    imag = diag_inverse[1].astype(F32)
    turn = ((0,), (0,))
    for block in range(ANC // COLS):
        keep = fill[0, block].astype(F32).astype(BF16)
        span = slice(block * COLS, (block + 1) * COLS)
        low_real, low_imag = lower[0, span, :] * keep, lower[1, span, :] * keep
        up_real, up_imag = upper[0, span, :], upper[1, span, :]
        real = real - mm(low_real, up_real, turn) + mm(low_imag, up_imag, turn)
        imag = imag - mm(low_real, up_imag, turn) - mm(low_imag, up_real, turn)
    out[0] = real.astype(BF16)
    out[1] = imag.astype(BF16)


def diag_block(fill, lower, upper, diag_inverse):
    return pl.pallas_call(
        diag_kernel,
        in_specs=[SMEM_SPEC] + [VMEM_SPEC] * 3,
        out_specs=VMEM_SPEC,
        out_shape=jax.ShapeDtypeStruct((2, COLS, COLS), BF16),
        compiler_params=params(),
        name="diag",
    )(fill, lower, upper, diag_inverse)


def turn_kernel(arrived, out):
    total = jnp.sum(arrived[...], axis=0)
    width = PLANE * CAP
    for n in range(PLANE):
        out[n] = total if n == 0 else pltpu.roll(total, width - n * CAP, 1)


def turn(arrived):
    return pl.pallas_call(
        turn_kernel,
        in_specs=[VMEM_SPEC],
        out_specs=VMEM_SPEC,
        out_shape=jax.ShapeDtypeStruct((PLANE, 8, PLANE * CAP), F32),
        compiler_params=params(),
        name="turn",
    )(arrived)


def place_kernel(arrived, onehot, *outs):
    width = PLANE * CAP
    line, lane = iota((8, width), 0), iota((8, width), 1)
    total = jnp.zeros((8, width), F32)
    for n in range(PLANE):
        piece = jnp.where(lane < CAP, arrived[n], 0.0)
        total = total + (piece if n == 0 else pltpu.roll(piece, n * CAP, 1))
    wide = jnp.concatenate([jnp.where((line >> 1) == px, total, 0.0) for px in range(NX)], axis=1)
    result = split_matmul(wide, onehot[...], ((1,), (0,)))
    for which in range(2):
        outs[which][...] = jnp.sum(
            jnp.where((iota((8, COLS), 0) & 1) == which, result, 0.0), axis=0, keepdims=True
        )


def place(arrived, onehot):
    return pl.pallas_call(
        place_kernel,
        in_specs=[VMEM_SPEC] * 2,
        out_specs=[VMEM_SPEC] * 2,
        out_shape=[jax.ShapeDtypeStruct((1, COLS), F32)] * 2,
        compiler_params=params(),
        name="place",
    )(arrived, onehot)


SIZES = {"ylo": 2, "core": 2, "x": NX, "yhi": NY, "z": NZ}


def shift(value, axis, by):
    size = SIZES[axis]
    return lax.ppermute(value, axis, [(n, (n + by) % size) for n in range(size)])


def all_of_z(value):
    pair = jnp.stack([value, shift(value, "z", 4)])
    return [pair, shift(pair, "z", 1), shift(pair, "z", -1), shift(pair, "z", 2)]


def body(ainv_anc, lower_panels, fill_pattern, diag_inverse, pole_weights, hamiltonian, margin, dft_column):
    pole = lax.axis_index("ylo") * 2 + lax.axis_index("core")
    grid = (lax.axis_index("x") * NY + lax.axis_index("yhi")) * NZ + lax.axis_index("z")
    index = jnp.stack([pole, grid]).astype(I32)
    lower, inverse = lower_panels[0], diag_inverse[0]
    shard = ainv_anc[0]

    table = dft_column.reshape(128, 128)
    *packed, slot_onehot = pack(index, table, margin, hamiltonian)
    z_4 = shift(shard, "z", 4)
    z_4, *packed = lax.optimization_barrier((z_4, *packed))

    near = jnp.stack([shard, z_4])
    packed = [value.reshape(PLANE, CAP, 2 * QUARTER) for value in packed]
    sent = [packed[0]] + [shift(packed[d], "x", d) for d in (1, 2, 3)]
    near_up, near_down, near_two = [shift(near, "z", d) for d in (1, -1, 2)]
    near, near_up, near_down, near_two, *sent = lax.optimization_barrier((near, near_up, near_down, near_two, *sent))

    first = jnp.concatenate([near, near_up])
    second = jnp.concatenate([jnp.concatenate([near_down, near_two]), first[..., PART:]], axis=-1)
    first = first[..., :PART]
    first_x = [first] + [shift(first, "x", d) for d in (1, 2, 3)]
    second_y = [second, shift(second, "yhi", 1)]
    arrived = lax.all_to_all(jnp.stack(sent, axis=1), ("yhi", "z"), split_axis=0, concat_axis=0, tiled=True)
    (first_x, second_y, arrived) = lax.optimization_barrier((first_x, second_y, arrived))

    first_y = shift(jnp.concatenate(first_x), "yhi", 1)
    second_all = jnp.concatenate(second_y)
    second_x = [shift(second_all, "x", d) for d in (1, 2, 3)]
    mine, column_onehot = unpack(index, table, arrived.reshape(SLOTS, 2 * QUARTER))
    mine_far = shift(mine, "ylo", 1)
    rhs, early, sums = start_rows(pole_weights, fill_pattern, lower, inverse, first_x + second_y)
    first_y, second_x, mine_far, early = lax.optimization_barrier((first_y, second_x, mine_far, early))

    mates = shift(jnp.stack([mine, mine_far]), "core", 1)
    mate, mate_far = mates[0], mates[1]
    upper, upper_again = upper_rows(index, fill_pattern, rhs, early, [first_y] + second_y + second_x)
    quarters = [mine, mine_far, mate, mate_far]
    slots = charge_slots(index, pole_weights, fill_pattern, lower, sums, quarters, upper_again, column_onehot)
    diag = diag_block(fill_pattern, lower, upper_again, inverse)
    sums = lax.all_to_all(slots, ("ylo", "core", "x"), split_axis=0, concat_axis=0, tiled=True)
    sums = lax.all_to_all(turn(sums), ("yhi", "z"), split_axis=0, concat_axis=0, tiled=True)
    charges, energy = place(sums, slot_onehot)
    return (upper[None], diag[None], charges.reshape(COLS), energy.reshape(COLS))


def solution(mesh):
    fine = jax.sharding.Mesh(mesh.devices.reshape(2, 2, NX, NY, NZ), ("ylo", "core", "x", "yhi", "z"))
    pole, grid = ("ylo", "core"), ("x", "yhi", "z")
    return jax.shard_map(
        body,
        mesh=fine,
        in_specs=(
            P(pole, None, grid, None),
            P(pole, None, None, grid),
            P(grid, None),
            P(pole, None, None, grid),
            P(pole, None),
            P(None, grid),
            P(None, grid),
            P(),
        ),
        out_specs=(
            P(pole, None, None, grid),
            P(pole, None, None, grid),
            P(grid),
            P(grid),
        ),
        check_vma=False,
    )
```

```python
import jax
import jax.numpy as jnp
from jax import lax
from jax.experimental import pallas as pl
from jax.experimental.pallas import tpu as pltpu
from jax.sharding import PartitionSpec as P

F32 = jnp.float32
BF16 = jnp.bfloat16
I32 = jnp.int32
NX, NY, NZ = 4, 2, 8
GROUPS = NX * NY * NZ
POLES = 4
CAP = 8
SLOTS = GROUPS * CAP
PLANE = NY * NZ
COLS = 256
ANC = 1024
ROWS = 1280
QUARTER = ROWS // POLES
SHARD = ANC // GROUPS
PART = 896
MIB = 1024 * 1024
SMEM_SPEC = pl.BlockSpec(memory_space=pltpu.SMEM)
VMEM_SPEC = pl.BlockSpec(memory_space=pltpu.VMEM)
HBM_SPEC = pl.BlockSpec(memory_space=pltpu.HBM)


def params(mib=16):
    return pltpu.CompilerParams(vmem_limit_bytes=mib * MIB)


def mm(a, b, contract=((1,), (0,))):
    return lax.dot_general(a, b, (contract, ((), ())), preferred_element_type=F32)


def iota(shape, dim):
    return lax.broadcasted_iota(I32, shape, dim)


def flag(condition):
    return jnp.where(condition, 1.0, 0.0).astype(BF16)


def split_matmul(values, onehot, contract):
    high = values.astype(BF16)
    rest = values - high.astype(F32)
    middle = rest.astype(BF16)
    low = (rest - middle.astype(F32)).astype(BF16)
    return mm(high, onehot, contract) + mm(middle, onehot, contract) + mm(low, onehot, contract)


def pack_kernel(index, dft, margin, hamiltonian, out0, out1, out2, out3, slot_onehot, both, sems):
    start = pl.multiple_of(index[0] * QUARTER, QUARTER)
    copies = [
        pltpu.make_async_copy(ref.at[pl.ds(start, QUARTER), :], both.at[pl.ds(n * QUARTER, QUARTER), :], sems.at[n])
        for n, ref in enumerate((margin, hamiltonian))
    ]
    for copy in copies:
        copy.start()
    entries = dft[...]
    side = entries.shape[0]
    hit = (entries >> 8) == index[1]
    row, col = iota((side, side), 0), iota((side, side), 1)
    hit_flag = flag(hit)
    rank = mm(hit_flag, flag(row < col))
    previous = mm(flag(((row & 1) == 1) & (col == row - 1)), hit_flag).astype(BF16)
    rank = rank + mm(previous, jnp.ones((side, side), BF16))
    place = ((entries & 255) + 1).astype(F32)
    pair = flag((iota((GROUPS, side), 1) >> 1) == iota((GROUPS, side), 0))
    target = (iota((GROUPS, COLS), 1) + 1).astype(F32)
    pieces = []
    for r in range(CAP):
        picked = jnp.where(hit & (rank == float(r)), place, 0.0).astype(BF16)
        local = jnp.sum(mm(pair, picked), axis=1, keepdims=True)
        pieces.append(flag(local == target))
    by_rank = jnp.concatenate(pieces, axis=0)
    s, t = iota((SLOTS, SLOTS), 0), iota((SLOTS, SLOTS), 1)
    order = flag((s & (CAP - 1)) * GROUPS + (s >> 3) == t)
    slot_onehot[...] = mm(order, by_rank).astype(BF16)
    for copy in copies:
        copy.wait()
    rows = both[...]
    x = index[1] >> 4
    for turn, out in enumerate((out0, out1, out2, out3)):
        first = pl.multiple_of(((x + turn) & (NX - 1)) * (PLANE * CAP), PLANE * CAP)
        out[...] = mm(slot_onehot[pl.ds(first, PLANE * CAP), :], rows, ((1,), (1,))).astype(BF16)


def pack(index, dft, margin, hamiltonian):
    return pl.pallas_call(
        pack_kernel,
        in_specs=[SMEM_SPEC, VMEM_SPEC, HBM_SPEC, HBM_SPEC],
        out_specs=[VMEM_SPEC] * (NX + 1),
        out_shape=[jax.ShapeDtypeStruct((PLANE * CAP, 2 * QUARTER), BF16)] * NX
        + [jax.ShapeDtypeStruct((SLOTS, COLS), BF16)],
        scratch_shapes=[pltpu.VMEM((2 * QUARTER, COLS), BF16), pltpu.SemaphoreType.DMA((2,))],
        compiler_params=params(62),
        name="pack",
    )(index, dft, margin, hamiltonian)


def unpack_kernel(index, dft, arrived, out, column_onehot):
    grid = index[1]
    group_row = jnp.concatenate([dft[pl.ds(2 * grid, 1), :], dft[pl.ds(2 * grid + 1, 1), :]], axis=1) >> 8
    above, across = iota((COLS, COLS), 0), iota((COLS, COLS), 1)
    group_col = jnp.sum(jnp.where(above == across, group_row, 0), axis=1, keepdims=True)
    rank = jnp.sum(jnp.where((group_col == group_row) & (above < across), 1, 0), axis=0, keepdims=True)
    place = iota((SLOTS, COLS), 0)
    column_onehot[...] = flag(place == group_row * CAP + rank)
    turn = ((grid >> 4) - (group_row >> 4)) & (NX - 1)
    slot = (group_row & (PLANE - 1)) * (NX * CAP) + turn * CAP + rank
    out[...] = mm(arrived[...], flag(place == slot), ((0,), (0,))).astype(BF16)


def unpack(index, dft, arrived):
    return pl.pallas_call(
        unpack_kernel,
        in_specs=[SMEM_SPEC] + [VMEM_SPEC] * 2,
        out_specs=[VMEM_SPEC] * 2,
        out_shape=[
            jax.ShapeDtypeStruct((2 * QUARTER, COLS), BF16),
            jax.ShapeDtypeStruct((SLOTS, COLS), BF16),
        ],
        compiler_params=params(),
        name="unpack",
    )(index, dft, arrived)


UP, DOWN = (0, 4, 1, 5), (7, 3, 2, 6)


def product(lefts, rhs):
    left, right = [mm(lefts(part), rhs) for part in range(2)]
    return right[:, COLS:] - left[:, :COLS], -left[:, COLS:] - right[:, :COLS]


def rows_of(refs, part, columns):
    return jnp.concatenate([ref[:, part, :, columns].reshape(-1, columns.stop - columns.start) for ref in refs], axis=0)


WHOLE, NEAR, REST = slice(0, ANC), slice(0, PART), slice(ANC, 2 * ANC - PART)


def start_kernel(weights, fill, lower, diag_inverse, *refs):
    first, second, (rhs, out, sums) = refs[:4], refs[4:6], refs[6:]
    for block in range(ANC // COLS):
        keep = fill[0, block].astype(F32).astype(BF16)
        span = slice(block * COLS, (block + 1) * COLS)
        for part in range(2):
            rhs[span, part * COLS : (part + 1) * COLS] = lower[part, span, :] * keep
    sums[...] = weights[0, 0] * diag_inverse[1].astype(F32) + weights[0, 1] * diag_inverse[0].astype(F32)
    rows = 0
    for group, columns in ((first, NEAR), (second, WHOLE)):
        real, imag = product(lambda part: rows_of(group, part, columns), rhs[columns, :])
        span = slice(rows, rows + real.shape[0])
        out[0, span, :] = real
        out[1, span, :] = imag
        rows = rows + real.shape[0]


def start_rows(weights, fill, lower, diag_inverse, pieces):
    rows = sum(value.shape[0] for value in pieces) * SHARD
    return pl.pallas_call(
        start_kernel,
        in_specs=[SMEM_SPEC] * 2 + [VMEM_SPEC] * (2 + len(pieces)),
        out_specs=[VMEM_SPEC] * 3,
        out_shape=[
            jax.ShapeDtypeStruct((ANC, 2 * COLS), BF16),
            jax.ShapeDtypeStruct((2, rows, COLS), F32),
            jax.ShapeDtypeStruct((COLS, COLS), F32),
        ],
        compiler_params=params(16),
        name="start",
    )(weights, fill, lower, diag_inverse, *pieces)


def upper_kernel(index, fill, rhs, early, first_y, second_0, second_y, second_1, second_2, second_3, *outs):
    grid = index[1]
    x, y, z = grid >> 4, (grid >> 3) & 1, grid & 7

    def scatter(real, imag, places):
        for n, (dx, dy, dz) in enumerate(places):
            px, py, pz = (x - dx) & (NX - 1), (y - dy) & (NY - 1), (z - dz) & (NZ - 1)
            here = pl.ds(pl.multiple_of(((px * NY + py) * NZ + pz) * SHARD, SHARD), SHARD)
            keep = fill[0, px].astype(F32)
            span = slice(n * SHARD, (n + 1) * SHARD)
            for part, value in enumerate((real, imag)):
                rows = (value[span] * keep).astype(BF16)
                for out in outs:
                    out[part, here, :] = rows

    def places(dxs, dys, dzs):
        return [(dx, dy, dz) for dx in dxs for dy in dys for dz in dzs]

    far = (second_1, second_2, second_3)
    own = NX * len(UP) * SHARD
    real, imag = product(lambda part: rows_of([second_0] + [ref.at[0:4] for ref in far], part, REST), rhs[PART:ANC, :])
    scatter(real + early[0, 0:own, :], imag + early[1, 0:own, :], places(range(NX), (0,), UP))
    scatter(early[0, own:, :], early[1, own:, :], places((0,), range(NY), DOWN))
    real, imag = product(lambda part: rows_of([second_y] + [ref.at[4:8] for ref in far], part, REST), rhs[PART:ANC, :])
    more_real, more_imag = product(lambda part: rows_of([first_y], part, NEAR), rhs[NEAR, :])
    scatter(real + more_real, imag + more_imag, places(range(NX), (1,), UP))
    real, imag = product(lambda part: rows_of(far, part, WHOLE), rhs[...])
    scatter(real, imag, places((1, 2, 3), range(NY), DOWN))


def upper_rows(index, fill, rhs, early, pieces):
    shape = jax.ShapeDtypeStruct((2, ANC, COLS), BF16)
    return pl.pallas_call(
        upper_kernel,
        in_specs=[SMEM_SPEC] * 2 + [VMEM_SPEC] * (2 + len(pieces)),
        out_specs=[VMEM_SPEC] * 2,
        out_shape=[shape, shape],
        compiler_params=params(20),
        name="upper",
    )(index, fill, rhs, early, *pieces)


def charge_kernel(index, weights, lower, sums, own, own_far, mate, mate_far, upper, onehot, slots, rows):
    pole, x = index[0], index[1] >> 4
    for bits, ref in ((0, own), (2, own_far), (1, mate), (3, mate_far)):
        start = pl.multiple_of((pole ^ bits) * QUARTER, QUARTER)
        for which in range(2):
            rows[which, pl.ds(start, QUARTER), :] = ref[which * QUARTER : (which + 1) * QUARTER, :]
    real, imag = weights[0, 0], weights[0, 1]
    nears = [rows[which, 0:COLS, :] for which in range(2)]
    totals = [jnp.sum(sums[...] * near.astype(F32), axis=0, keepdims=True) for near in nears]
    both = jnp.concatenate(nears, axis=1)
    for block in range(ANC // COLS):
        span = slice(block * COLS, (block + 1) * COLS)
        up_real, up_imag = upper[0, span, :].astype(F32), upper[1, span, :].astype(F32)
        to_direct = imag * up_real + real * up_imag
        to_cross = imag * up_imag - real * up_real
        direct = mm(lower[span, 0:COLS], both)
        cross = mm(lower[span, COLS:], both)
        for which in range(2):
            part = slice(which * COLS, (which + 1) * COLS)
            far = rows[which, (block + 1) * COLS : (block + 2) * COLS, :].astype(F32)
            term = to_direct * (far - direct[:, part]) + to_cross * cross[:, part]
            totals[which] = totals[which] + jnp.sum(term, axis=0, keepdims=True)
    line = iota((8, COLS), 0)
    values = jnp.where(line == 2 * x, totals[0], jnp.where(line == 2 * x + 1, totals[1], 0.0))
    result = split_matmul(values, onehot[...], ((1,), (1,)))
    width = PLANE * CAP
    for px in range(NX):
        for n in range(POLES):
            slots[n * NX + px] = result[:, px * width : (px + 1) * width]


def charge_slots(index, weights, lower, sums, quarters, upper, onehot):
    return pl.pallas_call(
        charge_kernel,
        in_specs=[SMEM_SPEC] * 2 + [VMEM_SPEC] * (4 + len(quarters)),
        out_specs=VMEM_SPEC,
        out_shape=jax.ShapeDtypeStruct((POLES * NX, 8, PLANE * CAP), F32),
        scratch_shapes=[pltpu.VMEM((2, ROWS, COLS), BF16)],
        compiler_params=params(24),
        name="charge",
    )(index, weights, lower, sums, *quarters, upper, onehot)


def diag_kernel(lower, upper, diag_inverse, out):
    real = diag_inverse[0].astype(F32)
    imag = diag_inverse[1].astype(F32)
    turn = ((0,), (0,))
    for block in range(ANC // COLS):
        span = slice(block * COLS, (block + 1) * COLS)
        low_real, low_imag = lower[span, 0:COLS], lower[span, COLS:]
        up_real, up_imag = upper[0, span, :], upper[1, span, :]
        real = real - mm(low_real, up_real, turn) + mm(low_imag, up_imag, turn)
        imag = imag - mm(low_real, up_imag, turn) - mm(low_imag, up_real, turn)
    out[0] = real.astype(BF16)
    out[1] = imag.astype(BF16)


def diag_block(lower, upper, diag_inverse):
    return pl.pallas_call(
        diag_kernel,
        in_specs=[VMEM_SPEC] * 3,
        out_specs=VMEM_SPEC,
        out_shape=jax.ShapeDtypeStruct((2, COLS, COLS), BF16),
        compiler_params=params(),
        name="diag",
    )(lower, upper, diag_inverse)


def turn_kernel(arrived, out):
    total = jnp.sum(arrived[...], axis=0)
    width = PLANE * CAP
    for n in range(PLANE):
        out[n] = total if n == 0 else pltpu.roll(total, width - n * CAP, 1)


def turn(arrived):
    return pl.pallas_call(
        turn_kernel,
        in_specs=[VMEM_SPEC],
        out_specs=VMEM_SPEC,
        out_shape=jax.ShapeDtypeStruct((PLANE, 8, PLANE * CAP), F32),
        compiler_params=params(),
        name="turn",
    )(arrived)


def place_kernel(arrived, onehot, *outs):
    width = PLANE * CAP
    line, lane = iota((8, width), 0), iota((8, width), 1)
    total = jnp.zeros((8, width), F32)
    for n in range(PLANE):
        piece = jnp.where(lane < CAP, arrived[n], 0.0)
        total = total + (piece if n == 0 else pltpu.roll(piece, n * CAP, 1))
    wide = jnp.concatenate([jnp.where((line >> 1) == px, total, 0.0) for px in range(NX)], axis=1)
    result = split_matmul(wide, onehot[...], ((1,), (0,)))
    for which in range(2):
        outs[which][...] = jnp.sum(
            jnp.where((iota((8, COLS), 0) & 1) == which, result, 0.0), axis=0, keepdims=True
        )


def place(arrived, onehot):
    return pl.pallas_call(
        place_kernel,
        in_specs=[VMEM_SPEC] * 2,
        out_specs=[VMEM_SPEC] * 2,
        out_shape=[jax.ShapeDtypeStruct((1, COLS), F32)] * 2,
        compiler_params=params(),
        name="place",
    )(arrived, onehot)


SIZES = {"ylo": 2, "core": 2, "x": NX, "yhi": NY, "z": NZ}


def shift(value, axis, by):
    size = SIZES[axis]
    return lax.ppermute(value, axis, [(n, (n + by) % size) for n in range(size)])


def all_of_z(value):
    pair = jnp.stack([value, shift(value, "z", 4)])
    return [pair, shift(pair, "z", 1), shift(pair, "z", -1), shift(pair, "z", 2)]


def body(ainv_anc, lower_panels, fill_pattern, diag_inverse, pole_weights, hamiltonian, margin, dft_column):
    pole = lax.axis_index("ylo") * 2 + lax.axis_index("core")
    grid = (lax.axis_index("x") * NY + lax.axis_index("yhi")) * NZ + lax.axis_index("z")
    index = jnp.stack([pole, grid]).astype(I32)
    lower, inverse = lower_panels[0], diag_inverse[0]
    shard = ainv_anc[0]

    table = dft_column.reshape(128, 128)
    *packed, slot_onehot = pack(index, table, margin, hamiltonian)
    z_4 = shift(shard, "z", 4)
    z_4, *packed = lax.optimization_barrier((z_4, *packed))

    near = jnp.stack([shard, z_4])
    packed = [value.reshape(PLANE, CAP, 2 * QUARTER) for value in packed]
    sent = [packed[0]] + [shift(packed[d], "x", d) for d in (1, 2, 3)]
    near_up, near_down, near_two = [shift(near, "z", d) for d in (1, -1, 2)]
    near, near_up, near_down, near_two, *sent = lax.optimization_barrier((near, near_up, near_down, near_two, *sent))

    first = jnp.concatenate([near, near_up])
    second = jnp.concatenate([jnp.concatenate([near_down, near_two]), first[..., PART:]], axis=-1)
    first = first[..., :PART]
    first_x = [first] + [shift(first, "x", d) for d in (1, 2, 3)]
    second_y = [second, shift(second, "yhi", 1)]
    arrived = lax.all_to_all(jnp.stack(sent, axis=1), ("yhi", "z"), split_axis=0, concat_axis=0, tiled=True)
    (first_x, second_y, arrived) = lax.optimization_barrier((first_x, second_y, arrived))

    first_y = shift(jnp.concatenate(first_x), "yhi", 1)
    second_all = jnp.concatenate(second_y)
    second_x = [shift(second_all, "x", d) for d in (1, 2, 3)]
    mine, column_onehot = unpack(index, table, arrived.reshape(SLOTS, 2 * QUARTER))
    mine_far = shift(mine, "ylo", 1)
    rhs, early, sums = start_rows(pole_weights, fill_pattern, lower, inverse, first_x + second_y)
    first_y, second_x, mine_far, early = lax.optimization_barrier((first_y, second_x, mine_far, early))

    mates = shift(jnp.stack([mine, mine_far]), "core", 1)
    mate, mate_far = mates[0], mates[1]
    upper, upper_again = upper_rows(index, fill_pattern, rhs, early, [first_y] + second_y + second_x)
    quarters = [mine, mine_far, mate, mate_far]
    slots = charge_slots(index, pole_weights, rhs, sums, quarters, upper_again, column_onehot)
    diag = diag_block(rhs, upper_again, inverse)
    sums = lax.all_to_all(slots, ("ylo", "core", "x"), split_axis=0, concat_axis=0, tiled=True)
    sums = lax.all_to_all(turn(sums), ("yhi", "z"), split_axis=0, concat_axis=0, tiled=True)
    charges, energy = place(sums, slot_onehot)
    return (upper[None], diag[None], charges.reshape(COLS), energy.reshape(COLS))


def solution(mesh):
    fine = jax.sharding.Mesh(mesh.devices.reshape(2, 2, NX, NY, NZ), ("ylo", "core", "x", "yhi", "z"))
    pole, grid = ("ylo", "core"), ("x", "yhi", "z")
    return jax.shard_map(
        body,
        mesh=fine,
        in_specs=(
            P(pole, None, grid, None),
            P(pole, None, None, grid),
            P(grid, None),
            P(pole, None, None, grid),
            P(pole, None),
            P(None, grid),
            P(None, grid),
            P(),
        ),
        out_specs=(
            P(pole, None, None, grid),
            P(pole, None, None, grid),
            P(grid),
            P(grid),
        ),
        check_vma=False,
    )
```

```python
import jax
import jax.numpy as jnp
from jax import lax
from jax.experimental import pallas as pl
from jax.experimental.pallas import tpu as pltpu
from jax.sharding import PartitionSpec as P

F32 = jnp.float32
BF16 = jnp.bfloat16
I32 = jnp.int32
NX, NY, NZ = 4, 2, 8
GROUPS = NX * NY * NZ
POLES = 4
CAP = 8
SLOTS = GROUPS * CAP
PLANE = NY * NZ
COLS = 256
ANC = 1024
ROWS = 1280
QUARTER = ROWS // POLES
SHARD = ANC // GROUPS
PART = 768
MIB = 1024 * 1024
SMEM_SPEC = pl.BlockSpec(memory_space=pltpu.SMEM)
VMEM_SPEC = pl.BlockSpec(memory_space=pltpu.VMEM)
HBM_SPEC = pl.BlockSpec(memory_space=pltpu.HBM)


def params(mib=16):
    return pltpu.CompilerParams(vmem_limit_bytes=mib * MIB)


def mm(a, b, contract=((1,), (0,))):
    return lax.dot_general(a, b, (contract, ((), ())), preferred_element_type=F32)


def iota(shape, dim):
    return lax.broadcasted_iota(I32, shape, dim)


def flag(condition):
    return jnp.where(condition, 1.0, 0.0).astype(BF16)


def split_matmul(values, onehot, contract):
    high = values.astype(BF16)
    rest = values - high.astype(F32)
    middle = rest.astype(BF16)
    low = (rest - middle.astype(F32)).astype(BF16)
    return mm(high, onehot, contract) + mm(middle, onehot, contract) + mm(low, onehot, contract)


def pack_kernel(index, dft, margin, hamiltonian, out0, out1, out2, out3, slot_onehot, both, sems):
    start = pl.multiple_of(index[0] * QUARTER, QUARTER)
    copies = [
        pltpu.make_async_copy(ref.at[pl.ds(start, QUARTER), :], both.at[pl.ds(n * QUARTER, QUARTER), :], sems.at[n])
        for n, ref in enumerate((margin, hamiltonian))
    ]
    for copy in copies:
        copy.start()
    entries = dft[...]
    side = entries.shape[0]
    hit = (entries >> 8) == index[1]
    row, col = iota((side, side), 0), iota((side, side), 1)
    hit_flag = flag(hit)
    rank = mm(hit_flag, flag(row < col))
    previous = mm(flag(((row & 1) == 1) & (col == row - 1)), hit_flag).astype(BF16)
    rank = rank + mm(previous, jnp.ones((side, side), BF16))
    place = ((entries & 255) + 1).astype(F32)
    pair = flag((iota((GROUPS, side), 1) >> 1) == iota((GROUPS, side), 0))
    target = (iota((GROUPS, COLS), 1) + 1).astype(F32)
    pieces = []
    for r in range(CAP):
        picked = jnp.where(hit & (rank == float(r)), place, 0.0).astype(BF16)
        local = jnp.sum(mm(pair, picked), axis=1, keepdims=True)
        pieces.append(flag(local == target))
    by_rank = jnp.concatenate(pieces, axis=0)
    s, t = iota((SLOTS, SLOTS), 0), iota((SLOTS, SLOTS), 1)
    order = flag((s & (CAP - 1)) * GROUPS + (s >> 3) == t)
    slot_onehot[...] = mm(order, by_rank).astype(BF16)
    for copy in copies:
        copy.wait()
    rows = both[...]
    x = index[1] >> 4
    for turn, out in enumerate((out0, out1, out2, out3)):
        first = pl.multiple_of(((x + turn) & (NX - 1)) * (PLANE * CAP), PLANE * CAP)
        out[...] = mm(slot_onehot[pl.ds(first, PLANE * CAP), :], rows, ((1,), (1,))).astype(BF16)


def pack(index, dft, margin, hamiltonian):
    return pl.pallas_call(
        pack_kernel,
        in_specs=[SMEM_SPEC, VMEM_SPEC, HBM_SPEC, HBM_SPEC],
        out_specs=[VMEM_SPEC] * (NX + 1),
        out_shape=[jax.ShapeDtypeStruct((PLANE * CAP, 2 * QUARTER), BF16)] * NX
        + [jax.ShapeDtypeStruct((SLOTS, COLS), BF16)],
        scratch_shapes=[pltpu.VMEM((2 * QUARTER, COLS), BF16), pltpu.SemaphoreType.DMA((2,))],
        compiler_params=params(62),
        name="pack",
    )(index, dft, margin, hamiltonian)


def unpack_kernel(index, dft, arrived, out, column_onehot):
    grid = index[1]
    group_row = jnp.concatenate([dft[pl.ds(2 * grid, 1), :], dft[pl.ds(2 * grid + 1, 1), :]], axis=1) >> 8
    above, across = iota((COLS, COLS), 0), iota((COLS, COLS), 1)
    group_col = jnp.sum(jnp.where(above == across, group_row, 0), axis=1, keepdims=True)
    rank = jnp.sum(jnp.where((group_col == group_row) & (above < across), 1, 0), axis=0, keepdims=True)
    place = iota((SLOTS, COLS), 0)
    column_onehot[...] = flag(place == group_row * CAP + rank)
    turn = ((grid >> 4) - (group_row >> 4)) & (NX - 1)
    slot = (group_row & (PLANE - 1)) * (NX * CAP) + turn * CAP + rank
    out[...] = mm(arrived[...], flag(place == slot), ((0,), (0,))).astype(BF16)


def unpack(index, dft, arrived):
    return pl.pallas_call(
        unpack_kernel,
        in_specs=[SMEM_SPEC] + [VMEM_SPEC] * 2,
        out_specs=[VMEM_SPEC] * 2,
        out_shape=[
            jax.ShapeDtypeStruct((2 * QUARTER, COLS), BF16),
            jax.ShapeDtypeStruct((SLOTS, COLS), BF16),
        ],
        compiler_params=params(),
        name="unpack",
    )(index, dft, arrived)


UP, DOWN = (0, 4, 1, 5), (7, 3, 2, 6)


def product(lefts, rhs):
    left, right = [mm(lefts(part), rhs) for part in range(2)]
    return right[:, COLS:] - left[:, :COLS], -left[:, COLS:] - right[:, :COLS]


def rows_of(refs, part, columns):
    return jnp.concatenate([ref[:, part, :, columns].reshape(-1, columns.stop - columns.start) for ref in refs], axis=0)


WHOLE, NEAR, REST = slice(0, ANC), slice(0, PART), slice(ANC, 2 * ANC - PART)


def start_kernel(weights, fill, lower, diag_inverse, *refs):
    first, second, (rhs, out, sums) = refs[:4], refs[4:6], refs[6:]
    for block in range(ANC // COLS):
        keep = fill[0, block].astype(F32).astype(BF16)
        span = slice(block * COLS, (block + 1) * COLS)
        for part in range(2):
            rhs[span, part * COLS : (part + 1) * COLS] = lower[part, span, :] * keep
    sums[...] = weights[0, 0] * diag_inverse[1].astype(F32) + weights[0, 1] * diag_inverse[0].astype(F32)
    rows = 0
    for group, columns in ((first, NEAR), (second, WHOLE)):
        real, imag = product(lambda part: rows_of(group, part, columns), rhs[columns, :])
        span = slice(rows, rows + real.shape[0])
        out[0, span, :] = real
        out[1, span, :] = imag
        rows = rows + real.shape[0]


def start_rows(weights, fill, lower, diag_inverse, pieces):
    rows = sum(value.shape[0] for value in pieces) * SHARD
    return pl.pallas_call(
        start_kernel,
        in_specs=[SMEM_SPEC] * 2 + [VMEM_SPEC] * (2 + len(pieces)),
        out_specs=[VMEM_SPEC] * 3,
        out_shape=[
            jax.ShapeDtypeStruct((ANC, 2 * COLS), BF16),
            jax.ShapeDtypeStruct((2, rows, COLS), F32),
            jax.ShapeDtypeStruct((COLS, COLS), F32),
        ],
        compiler_params=params(16),
        name="start",
    )(weights, fill, lower, diag_inverse, *pieces)


def upper_kernel(index, fill, rhs, early, first_y, second_0, second_y, second_1, second_2, second_3, *outs):
    grid = index[1]
    x, y, z = grid >> 4, (grid >> 3) & 1, grid & 7

    def scatter(real, imag, places):
        for n, (dx, dy, dz) in enumerate(places):
            px, py, pz = (x - dx) & (NX - 1), (y - dy) & (NY - 1), (z - dz) & (NZ - 1)
            here = pl.ds(pl.multiple_of(((px * NY + py) * NZ + pz) * SHARD, SHARD), SHARD)
            keep = fill[0, px].astype(F32)
            span = slice(n * SHARD, (n + 1) * SHARD)
            for part, value in enumerate((real, imag)):
                rows = (value[span] * keep).astype(BF16)
                for out in outs:
                    out[part, here, :] = rows

    def places(dxs, dys, dzs):
        return [(dx, dy, dz) for dx in dxs for dy in dys for dz in dzs]

    far = (second_1, second_2, second_3)
    own = NX * len(UP) * SHARD
    real, imag = product(lambda part: rows_of([second_0] + [ref.at[0:4] for ref in far], part, REST), rhs[PART:ANC, :])
    scatter(real + early[0, 0:own, :], imag + early[1, 0:own, :], places(range(NX), (0,), UP))
    scatter(early[0, own:, :], early[1, own:, :], places((0,), range(NY), DOWN))
    real, imag = product(lambda part: rows_of([second_y] + [ref.at[4:8] for ref in far], part, REST), rhs[PART:ANC, :])
    more_real, more_imag = product(lambda part: rows_of([first_y], part, NEAR), rhs[NEAR, :])
    scatter(real + more_real, imag + more_imag, places(range(NX), (1,), UP))
    real, imag = product(lambda part: rows_of(far, part, WHOLE), rhs[...])
    scatter(real, imag, places((1, 2, 3), range(NY), DOWN))


def upper_rows(index, fill, rhs, early, pieces):
    shape = jax.ShapeDtypeStruct((2, ANC, COLS), BF16)
    return pl.pallas_call(
        upper_kernel,
        in_specs=[SMEM_SPEC] * 2 + [VMEM_SPEC] * (2 + len(pieces)),
        out_specs=[VMEM_SPEC] * 2,
        out_shape=[shape, shape],
        compiler_params=params(20),
        name="upper",
    )(index, fill, rhs, early, *pieces)


def charge_kernel(index, weights, lower, sums, own, own_far, mate, mate_far, upper, onehot, slots, rows):
    pole, x = index[0], index[1] >> 4
    for bits, ref in ((0, own), (2, own_far), (1, mate), (3, mate_far)):
        start = pl.multiple_of((pole ^ bits) * QUARTER, QUARTER)
        for which in range(2):
            rows[which, pl.ds(start, QUARTER), :] = ref[which * QUARTER : (which + 1) * QUARTER, :]
    real, imag = weights[0, 0], weights[0, 1]
    nears = [rows[which, 0:COLS, :] for which in range(2)]
    totals = [jnp.sum(sums[...] * near.astype(F32), axis=0, keepdims=True) for near in nears]
    both = jnp.concatenate(nears, axis=1)
    for block in range(ANC // COLS):
        span = slice(block * COLS, (block + 1) * COLS)
        up_real, up_imag = upper[0, span, :].astype(F32), upper[1, span, :].astype(F32)
        to_direct = imag * up_real + real * up_imag
        to_cross = imag * up_imag - real * up_real
        direct = mm(lower[span, 0:COLS], both)
        cross = mm(lower[span, COLS:], both)
        for which in range(2):
            part = slice(which * COLS, (which + 1) * COLS)
            far = rows[which, (block + 1) * COLS : (block + 2) * COLS, :].astype(F32)
            term = to_direct * (far - direct[:, part]) + to_cross * cross[:, part]
            totals[which] = totals[which] + jnp.sum(term, axis=0, keepdims=True)
    line = iota((8, COLS), 0)
    values = jnp.where(line == 2 * x, totals[0], jnp.where(line == 2 * x + 1, totals[1], 0.0))
    result = split_matmul(values, onehot[...], ((1,), (1,)))
    width = PLANE * CAP
    for px in range(NX):
        for n in range(POLES):
            slots[n * NX + px] = result[:, px * width : (px + 1) * width]


def charge_slots(index, weights, lower, sums, quarters, upper, onehot):
    return pl.pallas_call(
        charge_kernel,
        in_specs=[SMEM_SPEC] * 2 + [VMEM_SPEC] * (4 + len(quarters)),
        out_specs=VMEM_SPEC,
        out_shape=jax.ShapeDtypeStruct((POLES * NX, 8, PLANE * CAP), F32),
        scratch_shapes=[pltpu.VMEM((2, ROWS, COLS), BF16)],
        compiler_params=params(24),
        name="charge",
    )(index, weights, lower, sums, *quarters, upper, onehot)


def diag_kernel(lower, upper, diag_inverse, out):
    real = diag_inverse[0].astype(F32)
    imag = diag_inverse[1].astype(F32)
    turn = ((0,), (0,))
    for block in range(ANC // COLS):
        span = slice(block * COLS, (block + 1) * COLS)
        low_real, low_imag = lower[span, 0:COLS], lower[span, COLS:]
        up_real, up_imag = upper[0, span, :], upper[1, span, :]
        real = real - mm(low_real, up_real, turn) + mm(low_imag, up_imag, turn)
        imag = imag - mm(low_real, up_imag, turn) - mm(low_imag, up_real, turn)
    out[0] = real.astype(BF16)
    out[1] = imag.astype(BF16)


def diag_block(lower, upper, diag_inverse):
    return pl.pallas_call(
        diag_kernel,
        in_specs=[VMEM_SPEC] * 3,
        out_specs=VMEM_SPEC,
        out_shape=jax.ShapeDtypeStruct((2, COLS, COLS), BF16),
        compiler_params=params(),
        name="diag",
    )(lower, upper, diag_inverse)


def turn_kernel(arrived, out):
    total = jnp.sum(arrived[...], axis=0)
    width = PLANE * CAP
    for n in range(PLANE):
        out[n] = total if n == 0 else pltpu.roll(total, width - n * CAP, 1)


def turn(arrived):
    return pl.pallas_call(
        turn_kernel,
        in_specs=[VMEM_SPEC],
        out_specs=VMEM_SPEC,
        out_shape=jax.ShapeDtypeStruct((PLANE, 8, PLANE * CAP), F32),
        compiler_params=params(),
        name="turn",
    )(arrived)


def place_kernel(arrived, onehot, *outs):
    width = PLANE * CAP
    line, lane = iota((8, width), 0), iota((8, width), 1)
    total = jnp.zeros((8, width), F32)
    for n in range(PLANE):
        piece = jnp.where(lane < CAP, arrived[n], 0.0)
        total = total + (piece if n == 0 else pltpu.roll(piece, n * CAP, 1))
    wide = jnp.concatenate([jnp.where((line >> 1) == px, total, 0.0) for px in range(NX)], axis=1)
    result = split_matmul(wide, onehot[...], ((1,), (0,)))
    for which in range(2):
        outs[which][...] = jnp.sum(
            jnp.where((iota((8, COLS), 0) & 1) == which, result, 0.0), axis=0, keepdims=True
        )


def place(arrived, onehot):
    return pl.pallas_call(
        place_kernel,
        in_specs=[VMEM_SPEC] * 2,
        out_specs=[VMEM_SPEC] * 2,
        out_shape=[jax.ShapeDtypeStruct((1, COLS), F32)] * 2,
        compiler_params=params(),
        name="place",
    )(arrived, onehot)


SIZES = {"ylo": 2, "core": 2, "x": NX, "yhi": NY, "z": NZ}


def shift(value, axis, by):
    size = SIZES[axis]
    return lax.ppermute(value, axis, [(n, (n + by) % size) for n in range(size)])


def all_of_z(value):
    pair = jnp.stack([value, shift(value, "z", 4)])
    return [pair, shift(pair, "z", 1), shift(pair, "z", -1), shift(pair, "z", 2)]


def body(ainv_anc, lower_panels, fill_pattern, diag_inverse, pole_weights, hamiltonian, margin, dft_column):
    pole = lax.axis_index("ylo") * 2 + lax.axis_index("core")
    grid = (lax.axis_index("x") * NY + lax.axis_index("yhi")) * NZ + lax.axis_index("z")
    index = jnp.stack([pole, grid]).astype(I32)
    lower, inverse = lower_panels[0], diag_inverse[0]
    shard = ainv_anc[0]

    table = dft_column.reshape(128, 128)
    *packed, slot_onehot = pack(index, table, margin, hamiltonian)
    z_4 = shift(shard, "z", 4)
    z_4, *packed = lax.optimization_barrier((z_4, *packed))

    near = jnp.stack([shard, z_4])
    packed = [value.reshape(PLANE, CAP, 2 * QUARTER) for value in packed]
    sent = [packed[0]] + [shift(packed[d], "x", d) for d in (1, 2, 3)]
    near_up, near_down, near_two = [shift(near, "z", d) for d in (1, -1, 2)]
    near, near_up, near_down, near_two, *sent = lax.optimization_barrier((near, near_up, near_down, near_two, *sent))

    first = jnp.concatenate([near, near_up])
    second = jnp.concatenate([jnp.concatenate([near_down, near_two]), first[..., PART:]], axis=-1)
    first = first[..., :PART]
    first_x = [first] + [shift(first, "x", d) for d in (1, 2, 3)]
    second_y = [second, shift(second, "yhi", 1)]
    arrived = lax.all_to_all(jnp.stack(sent, axis=1), ("yhi", "z"), split_axis=0, concat_axis=0, tiled=True)
    (first_x, second_y, arrived) = lax.optimization_barrier((first_x, second_y, arrived))

    first_y = shift(jnp.concatenate(first_x), "yhi", 1)
    second_all = jnp.concatenate(second_y)
    second_x = [shift(second_all, "x", d) for d in (1, 2, 3)]
    mine, column_onehot = unpack(index, table, arrived.reshape(SLOTS, 2 * QUARTER))
    mine_far = shift(mine, "ylo", 1)
    rhs, early, sums = start_rows(pole_weights, fill_pattern, lower, inverse, first_x + second_y)
    first_y, second_x, mine_far, early = lax.optimization_barrier((first_y, second_x, mine_far, early))

    mates = shift(jnp.stack([mine, mine_far]), "core", 1)
    mate, mate_far = mates[0], mates[1]
    upper, upper_again = upper_rows(index, fill_pattern, rhs, early, [first_y] + second_y + second_x)
    quarters = [mine, mine_far, mate, mate_far]
    slots = charge_slots(index, pole_weights, rhs, sums, quarters, upper_again, column_onehot)
    diag = diag_block(rhs, upper_again, inverse)
    sums = lax.all_to_all(slots, ("ylo", "core", "x"), split_axis=0, concat_axis=0, tiled=True)
    sums = lax.all_to_all(turn(sums), ("yhi", "z"), split_axis=0, concat_axis=0, tiled=True)
    charges, energy = place(sums, slot_onehot)
    return (upper[None], diag[None], charges.reshape(COLS), energy.reshape(COLS))


def solution(mesh):
    fine = jax.sharding.Mesh(mesh.devices.reshape(2, 2, NX, NY, NZ), ("ylo", "core", "x", "yhi", "z"))
    pole, grid = ("ylo", "core"), ("x", "yhi", "z")
    return jax.shard_map(
        body,
        mesh=fine,
        in_specs=(
            P(pole, None, grid, None),
            P(pole, None, None, grid),
            P(grid, None),
            P(pole, None, None, grid),
            P(pole, None),
            P(None, grid),
            P(None, grid),
            P(),
        ),
        out_specs=(
            P(pole, None, None, grid),
            P(pole, None, None, grid),
            P(grid),
            P(grid),
        ),
        check_vma=False,
    )
```
